32 devices in a mesh: row: 8 (over y, x, core), col: 4 (over z).
Axes of the slice: x: 2, y: 2, z: 4, core: 2. Of those that a mesh axis runs over, the one named last changes fastest.
Arguments:
- block_out: bfloat16 [384, 8192], P('row', 'col'), may hold values from -250 to 250
- stream_mid: bfloat16 [384, 8192], P('row', 'col'), may hold values from -250 to 250
- gate_pre: bfloat16 [384, 28672], P('row', 'col'), may hold values from -8 to 8
- up_pre: bfloat16 [384, 28672], P('row', 'col'), may hold values from -6 to 6
- final_gain: float32 [8192], P('col'), may hold values from 0.28 to 1.72
- mlp_gain: float32 [8192], P('col'), may hold values from 0.1 to 1.9
- value_weight: float32 [8192], P('col'), may hold values from -0.006629126 to 0.006629126
- returns: float32 [384], P('row'), may hold values from -6 to 6
- response_mask: int32 [384], P('row'), may hold values from 0 to 1, as said below
- w_gate: bfloat16 [8192, 28672], P('row', 'col'), may hold values from -0.0625 to 0.0625
- w_up: bfloat16 [8192, 28672], P('row', 'col'), may hold values from -0.0625 to 0.0625
- w_down: bfloat16 [28672, 8192], P('col', 'row'), may hold values from -0.03125 to 0.03125
Outputs:
- stream_mid_gradient: bfloat16 [384, 8192], P('row', 'col')
- d_w_down: float32 [28672, 8192], P('col', 'row')
The draws below stay inside these ranges and needn't reach their ends.
Inputs may be any that keep to these rules, and one draw needn't show every extreme that they name: `response_mask`: the last token of the micro-batch is a response token.
All inputs are finite; a program needn't handle non-finite values.
Results may differ from the reference program's by a relative error of at most 0.0075.
Values may be sent and summed in bfloat16 or wider, within the bound.
No kernel may reach another device: no remote copies, remote signals or barrier semaphores. Data moves between devices by JAX's collectives and lax.ppermute only.
A program may use at most 128 MiB of HBM per device.

```python
import math
import jax
import jax.numpy as jnp
from jax import lax

MODEL_WIDTH = 8192
FF = 28672
TOKENS = 384


def head_parts(key):
    gain_key, weight_key = jax.random.split(jax.random.fold_in(key, 5), 2)
    gain_values = 1.0 + 0.18 * jnp.clip(jax.random.normal(gain_key, (MODEL_WIDTH,), jnp.float32), -4.0, 4.0)
    weight_normal = jnp.clip(jax.random.normal(weight_key, (MODEL_WIDTH,), jnp.float32), -4.0, 4.0)
    return (gain_values, weight_normal)


def draw_stream(key, along_head):
    base_key = jax.random.fold_in(key, 0)
    col_key = jax.random.fold_in(key, 1)
    row_key = jax.random.fold_in(key, 2)
    sign_key = jax.random.fold_in(key, 4)
    position = jnp.arange(MODEL_WIDTH, dtype=jnp.float32) / MODEL_WIDTH
    col_scale = 10.0 ** position * jax.random.uniform(col_key, (MODEL_WIDTH,), jnp.float32, 0.7, 1.4)
    noise = jnp.clip(jax.random.normal(base_key, (TOKENS, MODEL_WIDTH), jnp.float32), -4.0, 4.0)
    row_scale = jnp.exp(jax.random.uniform(row_key, (TOKENS,), jnp.float32, 0.0, math.log(10.0)))
    field = noise * col_scale[None, :] / 8.0
    sign = (2 * jax.random.randint(sign_key, (TOKENS,), 0, 2, dtype=jnp.int32) - 1).astype(jnp.float32)
    field = field + 0.5 * sign[:, None] * along_head[None, :]
    return jnp.clip(field * row_scale[:, None], -250.0, 250.0).astype(jnp.bfloat16)


def draw_block_out(key, part):
    gain_values, weight_normal = head_parts(key)
    return draw_stream(jax.random.fold_in(key, 11), gain_values * weight_normal)


def draw_stream_mid(key, part):
    return draw_stream(jax.random.fold_in(key, 23), jnp.zeros((MODEL_WIDTH,), jnp.float32))


def draw_final_gain(key, part):
    gain_values, weight_normal = head_parts(key)
    return gain_values.astype(jnp.float32)


def draw_value_weight(key, part):
    gain_values, weight_normal = head_parts(key)
    return (weight_normal * (0.15 / math.sqrt(MODEL_WIDTH))).astype(jnp.float32)


def draw_response_mask(key, part):
    position = jnp.arange(TOKENS, dtype=jnp.int32)
    limit = 200 + 600 * position // max(TOKENS - 1, 1)
    ticket = jax.random.randint(jax.random.fold_in(key, 37), (TOKENS,), 0, 1000, dtype=jnp.int32)
    marked = (ticket < limit).astype(jnp.int32)
    return jnp.where(position == TOKENS - 1, 1, marked).astype(jnp.int32)


def block_levels(own_key, shape, cuts, smallest, largest):
    factor_of = 1.0
    for axis_at, shards_of in cuts:
        draws = jax.random.uniform(jax.random.fold_in(jax.random.fold_in(own_key, 6), axis_at), (shards_of,), jnp.float32, smallest / len(cuts), largest / len(cuts))
        factor_of = factor_of * jnp.repeat(jnp.exp(draws), shape[axis_at] // shards_of).reshape((-1,) + (1,) * (len(shape) - 1 - axis_at))
    return factor_of


def centred(rng, shape, deviation, reach, shards=(), held_as=jnp.bfloat16):
    values = jax.random.normal(rng, shape, jnp.float32) * deviation
    if len(shards) > 0:
        values = block_levels(rng, shape, shards, -0.22, 0.18) * values
    return jnp.clip(values, min=-reach, max=reach).astype(held_as)


def setup_inputs(seed: int = 0) -> dict:
    arg_keys = jax.random.split(jax.random.key(seed), 13)
    block_out = draw_block_out(jax.random.fold_in(arg_keys[12], 71), 0)
    stream_mid = draw_stream_mid(jax.random.fold_in(arg_keys[12], 71), 0)
    gate_pre = centred(arg_keys[2], (TOKENS, FF), 2.0, 8.0, ((0, 8), (1, 4)))
    up_pre = centred(arg_keys[3], (TOKENS, FF), 1.0, 6.0, ((0, 8), (1, 4)))
    final_gain = draw_final_gain(jax.random.fold_in(arg_keys[12], 71), 0)
    mlp_gain = jnp.clip(1.0 + 0.18 * jax.random.normal(arg_keys[5], (MODEL_WIDTH,), jnp.float32), 0.1, 1.9)
    value_weight = draw_value_weight(jax.random.fold_in(arg_keys[12], 71), 0)
    returns = centred(arg_keys[7], (TOKENS,), 1.0, 6.0, ((0, 8),), jnp.float32)
    response_mask = draw_response_mask(jax.random.fold_in(arg_keys[12], 71), 0)
    w_gate = centred(arg_keys[9], (MODEL_WIDTH, FF), MODEL_WIDTH ** -0.5, 0.0625, ((0, 8), (1, 4)))
    w_up = centred(arg_keys[10], (MODEL_WIDTH, FF), MODEL_WIDTH ** -0.5, 0.0625, ((0, 8), (1, 4)))
    w_down = centred(arg_keys[11], (FF, MODEL_WIDTH), FF ** -0.5, 0.03125, ((0, 4), (1, 8)))
    return dict(block_out=block_out, stream_mid=stream_mid, gate_pre=gate_pre, up_pre=up_pre, final_gain=final_gain, mlp_gain=mlp_gain, value_weight=value_weight, returns=returns, response_mask=response_mask, w_gate=w_gate, w_up=w_up, w_down=w_down)


epsilon = 1e-05

def contract(left, right, left_dim, right_dim):
    return lax.dot_general(left, right, (((left_dim,), (right_dim,)), ((), ())), preferred_element_type=jnp.float32)

def reference(block_out, stream_mid, gate_pre, up_pre, final_gain, mlp_gain, value_weight, returns, response_mask, w_gate, w_up, w_down):
    output_widened = block_out.astype(jnp.float32)
    middle_widened = stream_mid.astype(jnp.float32)
    output_inverse_root = lax.rsqrt(lax.optimization_barrier(jnp.mean(output_widened * output_widened, axis=1)) + epsilon)
    output_normalized_rows = output_widened * output_inverse_root[:, None]
    value_head = final_gain * value_weight
    value_estimate = lax.optimization_barrier(jnp.sum(output_normalized_rows * value_head[None, :], axis=1))
    live = response_mask.astype(jnp.float32)
    count = jnp.sum(live)
    dvalue = live * (value_estimate - returns) * (TOKENS * math.sqrt(MODEL_WIDTH) / count)
    adjoint_vector = value_head[None, :] * dvalue[:, None]
    inner_product = lax.optimization_barrier(jnp.sum(adjoint_vector * output_normalized_rows, axis=1))
    output_gradient = (output_inverse_root[:, None] * (adjoint_vector - output_normalized_rows * (inner_product / MODEL_WIDTH)[:, None])).astype(jnp.bfloat16)
    gate_wide = gate_pre.astype(jnp.float32)
    up_wide = up_pre.astype(jnp.float32)
    sigmoid_gate = jax.nn.sigmoid(gate_wide)
    hidden = (gate_wide * sigmoid_gate * up_wide).astype(jnp.bfloat16)
    d_w_down = contract(hidden, output_gradient, 0, 0)
    d_hidden = contract(output_gradient, w_down, 1, 1)
    d_gate = (d_hidden * up_wide * sigmoid_gate * (1.0 + gate_wide * (1.0 - sigmoid_gate))).astype(jnp.bfloat16)
    d_up = (d_hidden * gate_wide * sigmoid_gate).astype(jnp.bfloat16)
    d_normed = contract(d_gate, w_gate, 1, 1) + contract(d_up, w_up, 1, 1)
    middle_inverse_root = lax.rsqrt(lax.optimization_barrier(jnp.mean(middle_widened * middle_widened, axis=1)) + epsilon)
    middle_normalized_rows = middle_widened * middle_inverse_root[:, None]
    scaled_rows = d_normed * mlp_gain[None, :]
    middle_inner_product = lax.optimization_barrier(jnp.sum(scaled_rows * middle_normalized_rows, axis=1))
    stream_mid_gradient = output_gradient.astype(jnp.float32) + middle_inverse_root[:, None] * (scaled_rows - middle_normalized_rows * (middle_inner_product / MODEL_WIDTH)[:, None])
    return (stream_mid_gradient.astype(jnp.bfloat16), d_w_down)
```

```python
import math

import jax
import jax.numpy as jnp
from jax import lax
from jax.sharding import PartitionSpec as P

epsilon = 1e-05


def contract(left, right, left_dim, right_dim):
    return lax.dot_general(
        left, right, (((left_dim,), (right_dim,)), ((), ())), preferred_element_type=jnp.float32
    )


def exchange_pairs(rows, cols):
    k = rows // cols
    steps = []
    for s in range(k):
        pairs = []
        for r in range(rows):
            for c in range(cols):
                target = (k * c + (r + s) % k, r // k)
                pairs.append((r * cols + c, target[0] * cols + target[1]))
        steps.append(pairs)
    return steps


def local(
    block_out,
    stream_mid,
    gate_pre,
    up_pre,
    final_gain,
    mlp_gain,
    value_weight,
    returns,
    response_mask,
    w_gate,
    w_up,
    w_down,
):
    rows, cols = lax.axis_size("row"), lax.axis_size("col")
    row, col = lax.axis_index("row"), lax.axis_index("col")
    k = rows // cols
    both = ("row", "col")
    own, block = block_out.shape
    width = block * cols
    tile = width // rows
    tokens = own * rows
    steps = exchange_pairs(rows, cols)
    lane = row % k

    gate_all = lax.all_gather(gate_pre, "row", axis=0, tiled=True)
    up_all = lax.all_gather(up_pre, "row", axis=0, tiled=True)

    streams = jnp.stack([block_out, stream_mid]).reshape(2, own, k, tile)
    arrived = []
    for s in range(k):
        piece = lax.dynamic_index_in_dim(streams, (lane + s) % k, axis=2, keepdims=False)
        arrived.append(lax.ppermute(piece, both, steps[s]))
    held = jnp.stack(arrived)
    held = jnp.stack(
        [lax.dynamic_index_in_dim(held, (lane - p) % k, axis=0, keepdims=False) for p in range(k)], axis=1
    ).reshape(2, k * own, tile)
    out_tile = lax.all_gather(held[0], "col", axis=0, tiled=True)
    mid_tile = held[1]

    out_wide = block_out.astype(jnp.float32)
    mid_wide = stream_mid.astype(jnp.float32)
    head_local = final_gain * value_weight
    part = block // rows
    small = jnp.concatenate(
        [
            jnp.sum(out_wide * out_wide, axis=1),
            jnp.sum(out_wide * head_local[None, :], axis=1),
            jnp.sum(mid_wide * mid_wide, axis=1),
            returns,
            response_mask.astype(jnp.float32),
            lax.dynamic_slice_in_dim(head_local, row * part, part),
            lax.dynamic_slice_in_dim(mlp_gain, row * part, part),
        ]
    )
    gathered = lax.all_gather(small, both, axis=0, tiled=False).reshape(rows, cols, -1)
    sums = jnp.sum(gathered[:, :, : 3 * own], axis=1).reshape(rows, 3, own)
    square_out, head_sum, square_mid = (sums[:, i].reshape(-1) for i in range(3))
    targets = gathered[:, 0, 3 * own : 4 * own].reshape(-1)
    live = gathered[:, 0, 4 * own : 5 * own].reshape(-1)
    gains = gathered[:, :, 5 * own :].reshape(rows, cols, 2, part)
    gains = gains.transpose(2, 1, 0, 3).reshape(2, rows, tile)
    tile_gains = lax.dynamic_index_in_dim(gains, row, axis=1, keepdims=False)

    count = jnp.sum(live)
    out_root = lax.rsqrt(square_out / width + epsilon)
    mid_root = lax.rsqrt(square_mid / width + epsilon)
    value = out_root * head_sum
    dvalue = live * (value - targets) * (tokens * math.sqrt(width) / count)
    inner = dvalue * value / width

    def output_gradient(rows_of, root, scale, product, head):
        normalized = rows_of.astype(jnp.float32) * root[:, None]
        return (
            root[:, None] * (head[None, :] * scale[:, None] - normalized * product[:, None])
        ).astype(jnp.bfloat16)

    d_out = output_gradient(out_tile, out_root, dvalue, inner, tile_gains[0])

    partial = contract(d_out, w_down, 1, 1).astype(jnp.bfloat16)
    d_hidden = lax.psum(partial, "row").astype(jnp.float32)

    gate = gate_all.astype(jnp.float32)
    up = up_all.astype(jnp.float32)
    sig = jax.nn.sigmoid(gate)
    hidden = (gate * sig * up).astype(jnp.bfloat16)
    d_w_down = contract(hidden, d_out, 0, 0)
    d_gate = (d_hidden * up * sig * (1.0 + gate * (1.0 - sig))).astype(jnp.bfloat16)
    d_up = (d_hidden * gate * sig).astype(jnp.bfloat16)
    normed_part = contract(d_gate, w_gate, 1, 1) + contract(d_up, w_up, 1, 1)

    quarter = lax.psum_scatter(
        normed_part.astype(jnp.bfloat16), "col", scatter_dimension=0, tiled=True
    )
    quarter_root = lax.dynamic_slice_in_dim(mid_root, col * k * own, k * own)
    product_part = jnp.sum(
        quarter.astype(jnp.float32)
        * tile_gains[1][None, :]
        * (mid_tile.astype(jnp.float32) * quarter_root[:, None]),
        axis=1,
    )
    pieces = quarter.reshape(k, own, tile)
    back = []
    for s in range(k):
        piece = lax.dynamic_index_in_dim(pieces, (lane + s) % k, axis=0, keepdims=False)
        back.append(lax.ppermute(piece, both, steps[s]))
    back = jnp.stack(back)
    d_normed = jnp.concatenate(
        [lax.dynamic_index_in_dim(back, (lane - j) % k, axis=0, keepdims=False) for j in range(k)], axis=1
    ).astype(jnp.float32)
    products = lax.all_gather(product_part, both, axis=0, tiled=False).reshape(rows, tokens)
    products = jnp.sum(products, axis=0)

    def mine(values):
        return lax.dynamic_slice_in_dim(values, row * own, own)

    own_root = mine(mid_root)
    own_d_out = output_gradient(block_out, mine(out_root), mine(dvalue), mine(inner), head_local)
    gradient = own_d_out.astype(jnp.float32) + own_root[:, None] * (
        d_normed * mlp_gain[None, :] - mid_wide * own_root[:, None] * (mine(products) / width)[:, None]
    )
    return (gradient.astype(jnp.bfloat16), d_w_down)


def solution(mesh):
    placed = (
        P("row", "col"),
        P("row", "col"),
        P("row", "col"),
        P("row", "col"),
        P("col"),
        P("col"),
        P("col"),
        P("row"),
        P("row"),
        P("row", "col"),
        P("row", "col"),
        P("col", "row"),
    )
    return jax.shard_map(
        local,
        mesh=mesh,
        in_specs=placed,
        out_specs=(P("row", "col"), P("col", "row")),
        check_vma=False,
    )
```

```python
import functools
import math

import jax
import jax.numpy as jnp
from jax import lax
from jax.experimental import pallas as pl
from jax.experimental.pallas import tpu as pltpu
from jax.sharding import PartitionSpec as P

epsilon = 1e-05
LANES = 128
MIB = 1024 * 1024
F32 = jnp.float32
BF16 = jnp.bfloat16


def bits_of(n):
    return [1 << i for i in range(n.bit_length() - 1)]


def block_of(extent, most):
    best = LANES
    for size in range(LANES, most + 1, LANES):
        if extent % size == 0:
            best = size
    return best


def call(kernel, grid, ins, outs, shapes, scratch=(), limit=40, cost=None, aliases={}):
    return pl.pallas_call(
        kernel,
        grid=grid,
        in_specs=ins,
        out_specs=outs,
        out_shape=shapes,
        scratch_shapes=list(scratch),
        input_output_aliases=aliases,
        compiler_params=pltpu.CompilerParams(
            dimension_semantics=("arbitrary",) * len(grid), vmem_limit_bytes=limit * MIB
        ),
        cost_estimate=cost,
    )


def cost(flops, moved, special=0):
    return pl.CostEstimate(flops=int(flops), bytes_accessed=int(moved), transcendentals=int(special))


def whole(shape):
    return pl.BlockSpec(shape, lambda i: (0,) * len(shape))


def column(values, position):
    return values[:, position : position + 1]


def place(columns, rows):
    lane = lax.broadcasted_iota(jnp.int32, (rows, LANES), 1)
    out = jnp.zeros((rows, LANES), F32)
    for position, values in enumerate(columns):
        out = jnp.where(lane == position, values, out)
    return out


def sums_kernel(out_ref, mid_ref, gain_ref, weight_ref, sums_ref, head_ref):
    wide = out_ref[...].astype(F32)
    mid = mid_ref[...].astype(F32)
    head = gain_ref[...] * weight_ref[...]
    head_ref[...] = head
    sums_ref[...] = place(
        [
            jnp.sum(wide * wide, axis=1, keepdims=True),
            jnp.sum(wide * head, axis=1, keepdims=True),
            jnp.sum(mid * mid, axis=1, keepdims=True),
        ],
        out_ref.shape[0],
    )


def token_kernel(width, *refs):
    *parts, returns_ref, live_ref, token_ref = refs
    total = parts[0][...]
    for part in parts[1:]:
        total = total + part[...]
    root = lax.rsqrt(column(total, 0) / width + epsilon)
    mid_root = lax.rsqrt(column(total, 2) / width + epsilon)
    value = root * column(total, 1)
    live = live_ref[...].astype(F32)
    token_ref[...] = place(
        [root, value, live * (value - returns_ref[...]), live, mid_root], total.shape[0]
    )


def gradient_rows(rows_of, token, factor, width, head):
    root = column(token, 0)
    dvalue = column(token, 2) * factor
    product = dvalue * column(token, 1) / width
    normalized = rows_of * root
    return (root * (head * dvalue - normalized * product)).astype(BF16)


def out_kernel(width, rows, k, own, shift_ref, head_ref, *refs):
    tokens, pieces, (d_out_ref, factor_ref) = refs[:rows], refs[rows:-2], refs[-2:]
    held = jnp.concatenate([ref[...] for ref in tokens], axis=0)
    count = jnp.sum(column(held, 3), axis=0, keepdims=True)
    factor = (len(tokens) * own * math.sqrt(width)) / count
    factor_ref[...] = jnp.broadcast_to(factor, factor_ref.shape)
    head = head_ref[...]
    for d, piece in enumerate(pieces):
        at = lax.bitwise_xor(shift_ref[0], d)
        for s in range(k):
            rows_of = piece[s].astype(F32)
            token = tokens[0][...]
            for q in range(len(tokens)):
                token = jnp.where(at * k + s == q, tokens[q][...], token)
            d_out_ref[at * k + s] = gradient_rows(rows_of, token, factor, width, head)


def partial_kernel(d_out_ref, w_ref, send_ref, keep_ref):
    count, own, tile = d_out_ref.shape
    result = lax.dot_general(
        d_out_ref[...].reshape(count * own, tile),
        w_ref[...],
        (((1,), (1,)), ((), ())),
        preferred_element_type=F32,
    ).astype(BF16)
    result = result.reshape(count, own, -1)
    for q in range(count):
        (send_ref if q % 2 else keep_ref)[q // 2] = result[q]


def add_kernel(bit, keep_ref, came_ref, *outs):
    sent = kept = 0
    for q in range(keep_ref.shape[0]):
        total = (keep_ref[q].astype(F32) + came_ref[q].astype(F32)).astype(BF16)
        if len(outs) == 1:
            outs[0][...] = total
        elif q & bit:
            outs[0][sent] = total
            sent += 1
        else:
            outs[1][kept] = total
            kept += 1


def add(keep, came, bit):
    count, own, extent = keep.shape
    fb = block_of(extent, 1024)
    block = pl.BlockSpec((count, own, fb), lambda i: (0, 0, i))
    half = count // 2
    if count == 1:
        outs = [pl.BlockSpec((own, fb), lambda i: (0, i))]
        shapes = [jax.ShapeDtypeStruct((own, extent), BF16)]
    else:
        outs = [pl.BlockSpec((half, own, fb), lambda i: (0, 0, i))] * 2
        shapes = [jax.ShapeDtypeStruct((half, own, extent), BF16)] * 2
    return call(
        functools.partial(add_kernel, bit),
        (extent // fb,),
        [block, block],
        outs,
        shapes,
        cost=cost(count * own * extent, 6 * count * own * extent),
    )(keep, came)


def weight_kernel(d_out_ref, *refs):
    pieces, out_ref = refs[: d_out_ref.shape[0]], refs[-1]
    count, own, tile = d_out_ref.shape
    hidden = []
    for piece in pieces:
        gate, up = piece[0].astype(F32), piece[1].astype(F32)
        hidden.append((gate * jax.nn.sigmoid(gate) * up).astype(BF16))
    hidden = jnp.concatenate(hidden, axis=0)
    out_ref[...] = lax.dot_general(
        hidden,
        d_out_ref[...].reshape(count * own, tile),
        (((0,), (0,)), ((), ())),
        preferred_element_type=F32,
    )


def normed_kernel(first, last, k, shift_ref, w_gate_ref, w_up_ref, *refs):
    total = refs[-1]
    out_ref = refs[-2]
    refs = list(refs[:-2])
    before = None if first else refs.pop()
    count = len(refs) // 2
    pieces, grads = refs[:count], refs[count:]
    own = grads[0].shape[0]
    step = pl.program_id(0)

    d_gates, d_ups = [], []
    for piece, grad in zip(pieces, grads):
        gate, up, d_hidden = piece[0].astype(F32), piece[1].astype(F32), grad[...].astype(F32)
        sig = jax.nn.sigmoid(gate)
        through = d_hidden * sig
        d_gates.append((through * up * (1.0 + gate * (1.0 - sig))).astype(BF16))
        d_ups.append((through * gate).astype(BF16))
    contracted = (((1,), (1,)), ((), ()))
    result = lax.dot_general(
        jnp.concatenate(d_gates, axis=0), w_gate_ref[...], contracted, preferred_element_type=F32
    ) + lax.dot_general(
        jnp.concatenate(d_ups, axis=0), w_up_ref[...], contracted, preferred_element_type=F32
    )

    @pl.when(step == 0)
    def _():
        total[...] = result if first else before[...] + result

    @pl.when(step > 0)
    def _():
        total[...] += result

    @pl.when(step == pl.num_programs(0) - 1)
    def _():
        if not last:
            out_ref[...] = total[...]
        else:
            for d in range(count // k):
                at = lax.bitwise_xor(shift_ref[0], d)
                for s in range(k):
                    start = pl.multiple_of((at * k + s) * own, 16)
                    out_ref[d, s] = total[pl.ds(start, own), :].astype(BF16)


def local(
    block_out,
    stream_mid,
    gate_pre,
    up_pre,
    final_gain,
    mlp_gain,
    value_weight,
    returns,
    response_mask,
    w_gate,
    w_up,
    w_down,
):
    rows, cols = lax.axis_size("row"), lax.axis_size("col")
    row, col = lax.axis_index("row"), lax.axis_index("col")
    k = rows // cols
    own, block = block_out.shape
    width = block * cols
    tile = width // rows
    units = gate_pre.shape[1]
    lane = row % k
    shift = lax.bitwise_xor(row // k, col).astype(jnp.int32).reshape(1)

    def across(values, bit):
        return lax.ppermute(values, "row", [(r, r ^ bit) for r in range(rows)])

    def along(values, bit):
        return lax.ppermute(values, "col", [(c, c ^ bit) for c in range(cols)])

    def swap(values, s):
        pairs = [
            (r * cols + c, (k * c + ((r % k) ^ s)) * cols + r // k)
            for r in range(rows)
            for c in range(cols)
        ]
        return lax.ppermute(values, ("row", "col"), pairs)

    links = bits_of(rows)[1:]
    orders = [links, links[::-1]]

    sums, head = call(
        sums_kernel,
        (1,),
        [whole((own, block)), whole((own, block)), whole((1, block)), whole((1, block))],
        [whole((own, LANES)), whole((1, block))],
        [jax.ShapeDtypeStruct((own, LANES), F32), jax.ShapeDtypeStruct((1, block), F32)],
        cost=cost(own * block * 6, own * block * 4),
    )(block_out, stream_mid, final_gain[None, :], value_weight[None, :])

    tiles = block_out.reshape(own, k, tile)
    pieces = [
        swap(lax.dynamic_index_in_dim(tiles, lane ^ s, axis=1, keepdims=False), s) for s in range(k)
    ]
    head_tile = swap(
        lax.dynamic_index_in_dim(head.reshape(1, k, tile), lane, axis=1, keepdims=False), 0
    )
    sums_parts = [sums] + [along(sums, d) for d in range(1, cols)]
    pieces = jnp.stack(pieces)
    pieces = [pieces] + [along(pieces, d) for d in range(1, cols)]

    token = call(
        functools.partial(token_kernel, width),
        (1,),
        [whole((own, LANES))] * cols + [whole((own, 1))] * 2,
        whole((own, LANES)),
        jax.ShapeDtypeStruct((own, LANES), F32),
        cost=cost(own * LANES * 16, own * LANES * 4 * 8),
    )(*sums_parts, returns[:, None], response_mask[:, None])
    tokens = [token] + [across(token, q) for q in range(1, rows)]

    half = units // 2

    def gather(values, order):
        held = {0: values}
        for bit in order + [1]:
            held.update({q ^ bit: across(piece, bit) for q, piece in list(held.items())})
        return [held[q] for q in range(rows)]

    paired = [
        jnp.stack([gate_pre[:, h * half : (h + 1) * half], up_pre[:, h * half : (h + 1) * half]])
        for h in range(2)
    ]
    paired = [gather(paired[h], orders[h]) for h in range(2)]

    d_out, factor = call(
        functools.partial(out_kernel, width, rows, k, own),
        (1,),
        [pl.BlockSpec(memory_space=pltpu.SMEM), whole((1, tile))]
        + [whole((own, LANES))] * rows
        + [whole((k, own, tile))] * cols,
        [whole((rows, own, tile)), whole((8, LANES))],
        [jax.ShapeDtypeStruct((rows, own, tile), BF16), jax.ShapeDtypeStruct((8, LANES), F32)],
        cost=cost(rows * own * tile * 6, rows * own * tile * 4),
    )(shift, head_tile, *tokens, *pieces)

    fb = block_of(half, 512)
    blocks = half // fb
    grads = []
    for h in range(2):
        send, keep = call(
            partial_kernel,
            (blocks,),
            [
                whole((rows, own, tile)),
                pl.BlockSpec((fb, tile), lambda i, h=h: (h * blocks + i, 0)),
            ],
            [pl.BlockSpec((rows // 2, own, fb), lambda i: (0, 0, i))] * 2,
            [jax.ShapeDtypeStruct((rows // 2, own, half), BF16)] * 2,
            cost=cost(2 * rows * own * tile * half, 2 * half * tile + 2 * rows * own * half),
        )(d_out, w_down)
        remaining = [1] + orders[h]
        positions = bits_of(rows)
        for at, bit in enumerate(remaining):
            came = across(send, bit)
            positions.remove(bit)
            if not positions:
                (own_grad,) = add(keep, came, 0)
            else:
                send, keep = add(keep, came, 1 << positions.index(remaining[at + 1]))
        grads.append(gather(own_grad, orders[h]))

    d_w_down = None
    for h in range(2):
        ins = [whole((rows, own, tile))] + [pl.BlockSpec((2, own, fb), lambda i: (0, 0, i))] * rows
        args = [d_out, *paired[h]]
        aliases = {}
        if h:
            ins.append(pl.BlockSpec(memory_space=pl.ANY))
            args.append(d_w_down)
            aliases = {len(args) - 1: 0}
        d_w_down = call(
            weight_kernel,
            (blocks,),
            ins,
            pl.BlockSpec((fb, tile), lambda i, h=h: (h * blocks + i, 0)),
            jax.ShapeDtypeStruct((units, tile), F32),
            cost=cost(
                2 * rows * own * tile * half, 4 * half * tile + 4 * rows * own * half, rows * own * half
            ),
            aliases=aliases,
        )(*args)

    total = None
    for h in range(2):
        first, last = h == 0, h == 1
        weights = pl.BlockSpec((tile, fb), lambda i, h=h: (0, h * blocks + i))
        ins = (
            [pl.BlockSpec(memory_space=pltpu.SMEM), weights, weights]
            + [pl.BlockSpec((2, own, fb), lambda i: (0, 0, i))] * rows
            + [pl.BlockSpec((own, fb), lambda i: (0, i))] * rows
        )
        args = [shift, w_gate, w_up, *paired[h], *grads[h]]
        if not first:
            ins.append(whole((rows * own, tile)))
            args.append(total)
        shape = (cols, k, own, tile) if last else (rows * own, tile)
        total = call(
            functools.partial(normed_kernel, first, last, k),
            (blocks,),
            ins,
            whole(shape),
            jax.ShapeDtypeStruct(shape, BF16 if last else F32),
            scratch=[pltpu.VMEM((rows * own, tile), F32)],
            cost=cost(
                4 * rows * own * tile * half, 4 * half * tile + 6 * rows * own * half, rows * own * half
            ),
        )(*args)

    for bit in bits_of(cols):
        split = total.reshape(total.shape[0] // 2, 2, *total.shape[1:])
        total = (split[:, 0].astype(F32) + along(split[:, 1], bit).astype(F32)).astype(BF16)
    quarter = total[0]
    back = [swap(quarter[s], s).astype(F32) for s in range(k)]
    d_normed = jnp.concatenate(
        [
            functools.reduce(
                lambda other, s, j=j: jnp.where(lane ^ j == s, back[s], other), range(1, k), back[0]
            )
            for j in range(k)
        ],
        axis=1,
    )
    scaled = d_normed * mlp_gain[None, :]
    mid_root = column(token, 4)
    normalized = stream_mid.astype(F32) * mid_root
    product = jnp.sum(scaled * normalized, axis=1, keepdims=True)
    for bit in bits_of(cols):
        product = product + along(product, bit)
    own_d_out = gradient_rows(block_out.astype(F32), token, factor[0, 0], width, head)
    gradient = own_d_out.astype(F32) + mid_root * (scaled - normalized * (product / width))
    return (gradient.astype(BF16), d_w_down)


def solution(mesh):
    placed = (
        P("row", "col"),
        P("row", "col"),
        P("row", "col"),
        P("row", "col"),
        P("col"),
        P("col"),
        P("col"),
        P("row"),
        P("row"),
        P("row", "col"),
        P("row", "col"),
        P("col", "row"),
    )
    return jax.shard_map(
        local,
        mesh=mesh,
        in_specs=placed,
        out_specs=(P("row", "col"), P("col", "row")),
        check_vma=False,
    )
```

```python
import functools
import math

import jax
import jax.numpy as jnp
from jax import lax
from jax.experimental import pallas as pl
from jax.experimental.pallas import tpu as pltpu
from jax.sharding import PartitionSpec as P

epsilon = 1e-05
LANES = 128
MIB = 1024 * 1024
F32 = jnp.float32
BF16 = jnp.bfloat16


def bits_of(n):
    return [1 << i for i in range(n.bit_length() - 1)]


def block_of(extent, most):
    best = LANES
    for size in range(LANES, most + 1, LANES):
        if extent % size == 0:
            best = size
    return best


def call(kernel, grid, ins, outs, shapes, args, scratch=(), limit=40, cost=None, aliases={}, after=()):
    known, extra = len(ins), len(after)

    def body(*refs):
        kernel(*refs[:known], *refs[known + extra :])

    return pl.pallas_call(
        body,
        grid=grid,
        in_specs=list(ins) + [pl.BlockSpec(memory_space=pl.ANY)] * extra,
        out_specs=outs,
        out_shape=shapes,
        scratch_shapes=list(scratch),
        input_output_aliases=aliases,
        compiler_params=pltpu.CompilerParams(
            dimension_semantics=("arbitrary",) * len(grid), vmem_limit_bytes=limit * MIB
        ),
        cost_estimate=cost,
    )(*args, *after)


def cost(flops, moved, special=0):
    return pl.CostEstimate(flops=int(flops), bytes_accessed=int(moved), transcendentals=int(special))


def whole(shape):
    return pl.BlockSpec(shape, lambda i: (0,) * len(shape))


def column(values, position):
    return values[:, position : position + 1]


def place(columns, rows):
    lane = lax.broadcasted_iota(jnp.int32, (rows, LANES), 1)
    out = jnp.zeros((rows, LANES), F32)
    for position, values in enumerate(columns):
        out = jnp.where(lane == position, values, out)
    return out


def split_three(values):
    high = values.astype(BF16)
    rest = values - high.astype(F32)
    middle = rest.astype(BF16)
    return high, middle, (rest - middle.astype(F32)).astype(BF16)


def reverse_links(q, links):
    out = q & 1
    for i in range(links):
        out = out | (((q >> (1 + i)) & 1) << (links - i))
    return out


def other_core(j, links):
    return reverse_links(2 * j, links) | 1


def relative(place_ref, k, d):
    return lax.bitwise_xor(lax.bitwise_xor(lax.div(place_ref[0], k), place_ref[1]), d) * k


def label(place_ref, q, links):
    return jnp.where(lax.rem(place_ref[0], 2) == 1, reverse_links(q, links), q)


def tile_part(place_ref, k, s, tile):
    at = lax.bitwise_xor(lax.rem(place_ref[0], k), s)
    return pl.ds(pl.multiple_of(at * tile, LANES), tile)


def pack_kernel(place_ref, out_ref, gain_ref, weight_ref, *pieces):
    own, tile = out_ref.shape[0], pieces[0].shape[1]
    for s, piece in enumerate(pieces):
        part = tile_part(place_ref, len(pieces), s, tile)
        piece[0:own, :] = out_ref[:, part]
        if s == 0:
            head = gain_ref[:, part] * weight_ref[:, part]
            zero = jnp.zeros((1, tile), BF16)
            piece[own : own + 16, :] = jnp.concatenate([*split_three(head)] + [zero] * 13, axis=0)


def head_of(ref):
    wide = ref[...].astype(F32)
    return wide[0:1] + wide[1:2] + wide[2:3]


def turn(values):
    pad = jnp.zeros((LANES - values.shape[0], LANES), F32)
    return jnp.transpose(jnp.concatenate([values, pad], axis=0))


def sums_kernel(k, place_ref, head_ref, returns_ref, live_ref, *refs):
    pieces, sums_ref = refs[:-1], refs[-1]
    own = returns_ref.shape[1]
    head = head_of(head_ref)
    for d, piece in enumerate(pieces):
        at = relative(place_ref, k, d)
        for s in range(k):
            wide = piece[s].astype(F32)
            columns = place(
                [
                    jnp.sum(wide * wide, axis=1, keepdims=True),
                    jnp.sum(wide * head, axis=1, keepdims=True),
                ],
                own,
            )
            sums_ref[at + s] = turn(columns)[0:8]
    pad = jnp.zeros((1, LANES - own), F32)
    sublane = lax.broadcasted_iota(jnp.int32, (8, LANES), 0)
    targets = jnp.concatenate([returns_ref[...], pad], axis=1)
    live = jnp.concatenate([live_ref[...].astype(F32), pad], axis=1)
    mine = jnp.where(sublane == 2, targets, jnp.where(sublane == 3, live, 0.0))
    sums_ref[0] = sums_ref[0] + mine


def sum_rows_kernel(bit, sums_ref, came_ref, out_ref):
    for q in range(sums_ref.shape[0]):
        out_ref[q] = sums_ref[q] + came_ref[q ^ bit]


def gradient_rows(rows_of, token, head):
    root, dvalue, product = (column(token, i) for i in range(3))
    return (root * (head * dvalue - rows_of * root * product)).astype(BF16)


def out_kernel(width, k, bit, links, place_ref, head_ref, sums_ref, came_ref, *refs):
    pieces, (d_out_ref, token_ref, columns_ref) = refs[:-3], refs[-3:]
    rows, own = sums_ref.shape[0], d_out_ref.shape[1]
    head = head_of(head_ref)
    sums = [sums_ref[q] + came_ref[q ^ bit] for q in range(rows)]
    lives = functools.reduce(lambda a, b: a + b, [one[3:4] for one in sums])
    count = jnp.sum(lives, axis=1, keepdims=True)
    factor = (rows * own * math.sqrt(width)) / count
    for q, one in enumerate(sums):
        root = lax.rsqrt(one[0:1] / width + epsilon)
        value = root * one[1:2]
        dvalue = one[3:4] * (value - one[2:3]) * factor
        product = dvalue * value / width
        columns = jnp.concatenate([root, dvalue, product] + [jnp.zeros_like(root)] * 5, axis=0)
        columns_ref[q] = turn(columns)[0:own]
    token_ref[...] = columns_ref[0]
    for d, piece in enumerate(pieces):
        at = relative(place_ref, k, d)
        for s in range(k):
            d_out_ref[label(place_ref, at + s, links)] = gradient_rows(
                piece[s].astype(F32), columns_ref[at + s], head
            )


def partial_kernel(links, d_out_ref, w_ref, keep_ref, send_ref):
    count, own, tile = d_out_ref.shape
    result = lax.dot_general(
        d_out_ref[...].reshape(count * own, tile),
        w_ref[...],
        (((1,), (1,)), ((), ())),
        preferred_element_type=F32,
    ).astype(BF16)
    result = result.reshape(count, own, -1)
    for j in range(count // 2):
        keep_ref[j] = result[2 * j]
        send_ref[j] = result[other_core(j, links)]


def add_kernel(bit, keep_ref, came_ref, *outs):
    sent = kept = 0
    for q in range(keep_ref.shape[0]):
        total = (keep_ref[q].astype(F32) + came_ref[q].astype(F32)).astype(BF16)
        if len(outs) == 2 and q & bit:
            outs[1][sent] = total
            sent += 1
        else:
            outs[0][kept] = total
            kept += 1


def add(keep, came, bit, after=()):
    count, own, extent = keep.shape
    fb = block_of(extent, 2048 if count < 4 else 1024)
    block = pl.BlockSpec((count, own, fb), lambda i: (0, 0, i))
    parts = 2 if bit else 1
    out = pl.BlockSpec((count // parts, own, fb), lambda i: (0, 0, i))
    return call(
        functools.partial(add_kernel, bit),
        (extent // fb,),
        [block, block],
        [out] * parts,
        [jax.ShapeDtypeStruct((count // parts, own, extent), BF16)] * parts,
        [keep, came],
        cost=cost(count * own * extent, 6 * count * own * extent),
        after=after,
    )


def join_kernel(picks, *refs):
    for at, (i, j) in enumerate(picks):
        refs[-1][at] = refs[i][j]


def join(arrays, picks, after=()):
    own, extent = arrays[0].shape[1:]
    fb = block_of(extent, 1024)
    return call(
        functools.partial(join_kernel, picks),
        (extent // fb,),
        [pl.BlockSpec((array.shape[0], own, fb), lambda i: (0, 0, i)) for array in arrays],
        pl.BlockSpec((len(picks), own, fb), lambda i: (0, 0, i)),
        jax.ShapeDtypeStruct((len(picks), own, extent), BF16),
        arrays,
        cost=cost(0, 4 * len(picks) * own * extent),
        after=after,
    )


def every(*arrays):
    return [(i, j) for i, array in enumerate(arrays) for j in range(array.shape[0])]


def stack_kernel(*refs):
    for at, ref in enumerate(refs[:-1]):
        refs[-1][at] = ref[...]


def stack(arrays, own):
    extent = arrays[0].shape[1]
    fb = block_of(extent, 1024)
    return call(
        stack_kernel,
        (extent // fb,),
        [pl.BlockSpec((own, fb), lambda i: (0, i))] * len(arrays),
        pl.BlockSpec((len(arrays), own, fb), lambda i: (0, 0, i)),
        jax.ShapeDtypeStruct((len(arrays), own, extent), BF16),
        arrays,
        cost=cost(0, 4 * len(arrays) * own * extent),
    )


def weight_kernel(links, d_out_ref, mine_ref, other_ref, *refs):
    out_ref, done_ref = refs[-2:]
    count, own, tile = d_out_ref.shape
    hidden = [None] * count
    for j in range(count // 2):
        for ref, position in ((mine_ref, 2 * j), (other_ref, other_core(j, links))):
            gate, up = ref[2 * j].astype(F32), ref[2 * j + 1].astype(F32)
            hidden[position] = (gate * jax.nn.sigmoid(gate) * up).astype(BF16)
    out_ref[...] = lax.dot_general(
        jnp.concatenate(hidden, axis=0),
        d_out_ref[...].reshape(count * own, tile),
        (((0,), (0,)), ((), ())),
        preferred_element_type=F32,
    )
    done_ref[...] = jnp.zeros_like(done_ref)


def normed_kernel(links, first, last, k, place_ref, w_gate_ref, w_up_ref, mine_ref, other_ref, *refs):
    (mine_grad, other_grad), (out_ref, total) = refs[:2], refs[-2:]
    before = None if first else refs[2]
    count, own = 2 * mine_grad.shape[0], mine_grad.shape[1]
    step = pl.program_id(0)

    d_gates, d_ups = [None] * count, [None] * count
    for j in range(count // 2):
        for ref, grad, position in (
            (mine_ref, mine_grad, 2 * j),
            (other_ref, other_grad, other_core(j, links)),
        ):
            gate, up = ref[2 * j].astype(F32), ref[2 * j + 1].astype(F32)
            sig = jax.nn.sigmoid(gate)
            through = grad[j].astype(F32) * sig
            d_gates[position] = (through * up * (1.0 + gate * (1.0 - sig))).astype(BF16)
            d_ups[position] = (through * gate).astype(BF16)
    contracted = (((1,), (1,)), ((), ()))
    result = lax.dot_general(
        jnp.concatenate(d_gates, axis=0), w_gate_ref[...], contracted, preferred_element_type=F32
    ) + lax.dot_general(
        jnp.concatenate(d_ups, axis=0), w_up_ref[...], contracted, preferred_element_type=F32
    )

    @pl.when(step == 0)
    def _():
        total[...] = result if first else before[...] + result

    @pl.when(step > 0)
    def _():
        total[...] += result

    @pl.when(step == pl.num_programs(0) - 1)
    def _():
        if not last:
            out_ref[...] = total[...]
        else:
            for d in range(count // k):
                at = relative(place_ref, k, d)
                for s in range(k):
                    start = pl.multiple_of(label(place_ref, at + s, links) * own, 16)
                    out_ref[d * k + s] = total[pl.ds(start, own), :].astype(BF16)


def product_kernel(k, place_ref, mid_ref, gain_ref, *refs):
    backs, sums_ref = refs[:-1], refs[-1]
    own, tile = backs[0].shape
    products = squares = jnp.zeros((own, 1), F32)
    for s, back in enumerate(backs):
        part = tile_part(place_ref, k, s, tile)
        middle = mid_ref[:, part].astype(F32)
        products = products + jnp.sum(
            back[...].astype(F32) * gain_ref[:, part] * middle, axis=1, keepdims=True
        )
        squares = squares + jnp.sum(middle * middle, axis=1, keepdims=True)
    sums_ref[...] = place([products, squares], own)


def pair_kernel(first_ref, second_ref, out_ref):
    out_ref[...] = first_ref[...] + second_ref[...]


def result_kernel(width, k, place_ref, block_ref, mid_ref, norm_ref, weight_ref, gain_ref, token_ref, *refs):
    (sums_ref, came_ref), backs, out_ref = refs[:2], refs[2:-1], refs[-1]
    tile = backs[0].shape[1]
    sums = sums_ref[...] + came_ref[...]
    root = lax.rsqrt(column(sums, 1) / width + epsilon)
    product = column(sums, 0) * root / width
    for s, back in enumerate(backs):
        part = tile_part(place_ref, k, s, tile)
        own_d_out = gradient_rows(
            block_ref[:, part].astype(F32), token_ref[...], norm_ref[:, part] * weight_ref[:, part]
        )
        scaled = back[...].astype(F32) * gain_ref[:, part]
        normalized = mid_ref[:, part].astype(F32) * root
        out_ref[:, part] = (own_d_out.astype(F32) + root * (scaled - normalized * product)).astype(BF16)


def local(
    block_out,
    stream_mid,
    gate_pre,
    up_pre,
    final_gain,
    mlp_gain,
    value_weight,
    returns,
    response_mask,
    w_gate,
    w_up,
    w_down,
):
    rows, cols = lax.axis_size("row"), lax.axis_size("col")
    k = rows // cols
    own, block = block_out.shape
    width = block * cols
    tile = width // rows
    units = gate_pre.shape[1]
    where = jnp.stack([lax.axis_index("row"), lax.axis_index("col")]).astype(jnp.int32)
    smem = pl.BlockSpec(memory_space=pltpu.SMEM)
    final_gain, mlp_gain, value_weight = final_gain[None, :], mlp_gain[None, :], value_weight[None, :]

    link_bits = bits_of(rows)[1:]
    links = len(link_bits)

    def across(values, bit):
        return lax.ppermute(values, "row", [(r, r ^ bit) for r in range(rows)])

    def linked(values, i):
        pairs = [(r, r ^ link_bits[links - 1 - i if r % 2 else i]) for r in range(rows)]
        return lax.ppermute(values, "row", pairs)

    def along(values, bit):
        return lax.ppermute(values, "col", [(c, c ^ bit) for c in range(cols)])

    def swap(values, s):
        pairs = [
            (r * cols + c, (k * c + ((r % k) ^ s)) * cols + r // k)
            for r in range(rows)
            for c in range(cols)
        ]
        return lax.ppermute(values, ("row", "col"), pairs)

    paired = stack([gate_pre, up_pre], own)
    hop_a = linked(paired, 0)
    gate_b = linked(gate_pre[None], 1)

    shapes = [(own + 16 * (s == 0), tile) for s in range(k)]
    packed = call(
        pack_kernel,
        (1,),
        [smem, whole((own, block)), whole((1, block)), whole((1, block))],
        [whole(shape) for shape in shapes],
        [jax.ShapeDtypeStruct(shape, BF16) for shape in shapes],
        [where, block_out, final_gain, value_weight],
        cost=cost(own * block, own * block * 4),
    )
    swapped = [swap(packed[s], s) for s in range(k)]
    pieces = stack(swapped, own)
    pieces = [pieces] + [along(pieces, d) for d in range(1, cols)]
    head_spec = pl.BlockSpec((16, tile), lambda i: (own // 16, 0))

    more = join([paired, hop_a], [(0, 1), (1, 0), (1, 1)], after=pieces + [gate_b])
    piece_specs = [whole((k, own, tile))] * cols
    sums = call(
        functools.partial(sums_kernel, k),
        (1,),
        [smem, head_spec, whole((1, own)), whole((1, own))] + piece_specs,
        whole((rows, 8, LANES)),
        jax.ShapeDtypeStruct((rows, 8, LANES), F32),
        [where, swapped[0], returns[None, :], response_mask[None, :], *pieces],
        cost=cost(rows * own * tile * 4, rows * own * tile * 2),
        after=[more],
    )
    more_b = linked(more, 1)
    for bit in bits_of(rows)[:-1]:
        sums = call(
            functools.partial(sum_rows_kernel, bit),
            (1,),
            [whole((rows, 8, LANES))] * 2,
            whole((rows, 8, LANES)),
            jax.ShapeDtypeStruct((rows, 8, LANES), F32),
            [sums, across(sums, bit)],
            cost=cost(rows * 8 * LANES, rows * 8 * LANES * 12),
        )
    bit = bits_of(rows)[-1]
    d_out, token = call(
        functools.partial(out_kernel, width, k, bit, links),
        (1,),
        [smem, head_spec] + [whole((rows, 8, LANES))] * 2 + piece_specs,
        [whole((rows, own, tile)), whole((own, LANES))],
        [jax.ShapeDtypeStruct((rows, own, tile), BF16), jax.ShapeDtypeStruct((own, LANES), F32)],
        [where, swapped[0], sums, across(sums, bit), *pieces],
        scratch=[pltpu.VMEM((rows, own, LANES), F32)],
        cost=cost(rows * own * tile * 6, rows * own * tile * 4),
    )

    lines = units // LANES
    sizes = [lines * 5 // 14, lines * 5 // 14]
    sizes = [size * LANES for size in sizes + [lines - sum(sizes)]]
    chunks = [(sum(sizes[:i]), size) for i, size in enumerate(sizes)]
    grads, partial_sums = [], []
    for start, extent in chunks:
        fb = block_of(math.gcd(start, extent), 1024)
        keep, send = call(
            functools.partial(partial_kernel, links),
            (extent // fb,),
            [
                whole((rows, own, tile)),
                pl.BlockSpec((fb, tile), lambda i, f=start // fb: (f + i, 0)),
            ],
            [pl.BlockSpec((rows // 2, own, fb), lambda i: (0, 0, i))] * 2,
            [jax.ShapeDtypeStruct((rows // 2, own, extent), BF16)] * 2,
            [d_out, w_down],
            cost=cost(2 * rows * own * tile * extent, 2 * extent * tile + 2 * rows * own * extent),
        )
        partial_sums.append(send)
        received = across(send, 1)
        for i in range(links):
            keep, send = add(keep, received, 1)
            received = linked(send, i)
        (keep,) = add(keep, received, 0)
        for i in range(links - 1):
            came = linked(keep, i)
            keep = join([keep, came], every(keep, came))
        grads.append((keep, linked(keep, links - 1)))

    mine = join(
        [paired, hop_a, gate_b, more_b],
        every(paired, hop_a) + [(2, 0)] + [(3, j) for j in range(3)],
        after=partial_sums[1:2],
    )
    for i in range(2, links):
        came = linked(mine, i)
        mine = join([mine, came], every(mine, came))
    gathered = [mine, across(mine, 1)]

    total = None
    count = rows // 2
    for number, (start, extent) in enumerate(chunks):
        first, last = number == 0, number == len(chunks) - 1
        fb = block_of(math.gcd(start, extent), 1024)
        weights = pl.BlockSpec((tile, fb), lambda i, f=start // fb: (0, f + i))
        ins = (
            [smem, weights, weights]
            + [pl.BlockSpec((rows, own, fb), lambda i, f=start // fb: (0, 0, f + i))] * 2
            + [pl.BlockSpec((count, own, fb), lambda i: (0, 0, i))] * 2
        )
        keep, came = grads[number]
        mine = join([keep, came], every(keep, came), after=[total] if last else ())
        args = [where, w_gate, w_up, *gathered, mine, across(mine, 1)]
        if not first:
            ins.append(whole((rows * own, tile)))
            args.append(total)
        shape = (rows, own, tile) if last else (rows * own, tile)
        total = call(
            functools.partial(normed_kernel, links, first, last, k),
            (extent // fb,),
            ins,
            whole(shape),
            jax.ShapeDtypeStruct(shape, BF16 if last else F32),
            args,
            scratch=[pltpu.VMEM((rows * own, tile), F32)],
            limit=56,
            cost=cost(
                4 * rows * own * tile * extent,
                4 * extent * tile + 6 * rows * own * extent,
                rows * own * extent,
            ),
        )

    half = units // 2
    fb = block_of(half, 1024)
    blocks = half // fb
    d_w_down = None
    col_bits = bits_of(cols)
    for at, bit in enumerate(col_bits):
        n = total.shape[0] // (2 * k)
        split = total.reshape(n, 2, k, own, tile)
        keep, send = (split[:, side].reshape(n * k, own, tile) for side in range(2))
        received = along(send, bit)
        done = ()
        if at < 2:
            ins = [whole((rows, own, tile))] + [
                pl.BlockSpec((rows, own, fb), lambda i, at=at: (0, 0, at * blocks + i))
            ] * 2
            args = [d_out, *gathered]
            aliases = {}
            if at:
                ins.append(pl.BlockSpec(memory_space=pl.ANY))
                args.append(d_w_down)
                aliases = {len(args) - 1: 0}
            d_w_down, done = call(
                functools.partial(weight_kernel, links),
                (blocks,),
                ins,
                [pl.BlockSpec((fb, tile), lambda i, at=at: (at * blocks + i, 0)), whole((8, LANES))],
                [jax.ShapeDtypeStruct((units, tile), F32), jax.ShapeDtypeStruct((8, LANES), F32)],
                args,
                cost=cost(
                    2 * rows * own * tile * half,
                    4 * half * tile + 4 * rows * own * half,
                    rows * own * half,
                ),
                aliases=aliases,
                after=[total],
                limit=56,
            )
            done = (done,)
        (total,) = add(keep, received, 0, after=done)

    backs = [swap(total[s], s) for s in range(k)]
    row_spec, gain_spec = whole((own, block)), whole((1, block))
    sums_spec, back_specs = whole((own, LANES)), [whole((own, tile))] * k
    sums = call(
        functools.partial(product_kernel, k),
        (1,),
        [smem, row_spec, gain_spec] + back_specs,
        sums_spec,
        jax.ShapeDtypeStruct((own, LANES), F32),
        [where, stream_mid, mlp_gain, *backs],
        cost=cost(own * block * 5, own * block * 4),
    )
    for bit in col_bits[:-1]:
        sums = call(
            pair_kernel,
            (1,),
            [sums_spec] * 2,
            sums_spec,
            jax.ShapeDtypeStruct((own, LANES), F32),
            [sums, along(sums, bit)],
            cost=cost(own * LANES, own * LANES * 12),
        )
    gradient = call(
        functools.partial(result_kernel, width, k),
        (1,),
        [smem, row_spec, row_spec] + [gain_spec] * 3 + [sums_spec] * 3 + back_specs,
        row_spec,
        jax.ShapeDtypeStruct((own, block), BF16),
        [where, block_out, stream_mid, final_gain, value_weight, mlp_gain, token, sums]
        + [along(sums, col_bits[-1]), *backs],
        cost=cost(own * block * 14, own * block * 8),
    )
    return (gradient, d_w_down)


def solution(mesh):
    placed = (
        P("row", "col"),
        P("row", "col"),
        P("row", "col"),
        P("row", "col"),
        P("col"),
        P("col"),
        P("col"),
        P("row"),
        P("row"),
        P("row", "col"),
        P("row", "col"),
        P("col", "row"),
    )
    return jax.shard_map(
        local,
        mesh=mesh,
        in_specs=placed,
        out_specs=(P("row", "col"), P("col", "row")),
        check_vma=False,
    )
```

```python
import functools
import math

import jax
import jax.numpy as jnp
from jax import lax
from jax.experimental import pallas as pl
from jax.experimental.pallas import tpu as pltpu
from jax.sharding import PartitionSpec as P

epsilon = 1e-05
LANES = 128
MIB = 1024 * 1024
F32 = jnp.float32
BF16 = jnp.bfloat16


def bits_of(n):
    return [1 << i for i in range(n.bit_length() - 1)]


def block_of(extent, most):
    best = LANES
    for size in range(LANES, most + 1, LANES):
        if extent % size == 0:
            best = size
    return best


ordered = []


def call(kernel, grid, ins, outs, shapes, args, scratch=(), limit=32, cost=None, aliases={}, after=()):
    after = list(after) + ordered[-1:]
    known, extra = len(ins), len(after)

    def body(*refs):
        kernel(*refs[:known], *refs[known + extra :])

    result = pl.pallas_call(
        body,
        grid=grid,
        in_specs=list(ins) + [pl.BlockSpec(memory_space=pl.ANY)] * extra,
        out_specs=outs,
        out_shape=shapes,
        scratch_shapes=list(scratch),
        input_output_aliases=aliases,
        compiler_params=pltpu.CompilerParams(
            dimension_semantics=("arbitrary",) * len(grid), vmem_limit_bytes=limit * MIB
        ),
        cost_estimate=cost,
    )(*args, *after)
    ordered[:] = jax.tree.leaves(result)[-1:]
    return result


def cost(flops, moved, special=0):
    return pl.CostEstimate(flops=int(flops), bytes_accessed=int(moved), transcendentals=int(special))


def whole(shape):
    return pl.BlockSpec(shape, lambda i: (0,) * len(shape))


def column(values, position):
    return values[:, position : position + 1]


def place(columns, rows):
    lane = lax.broadcasted_iota(jnp.int32, (rows, LANES), 1)
    out = jnp.zeros((rows, LANES), F32)
    for position, values in enumerate(columns):
        out = jnp.where(lane == position, values, out)
    return out


def split_three(values):
    high = values.astype(BF16)
    rest = values - high.astype(F32)
    middle = rest.astype(BF16)
    return high, middle, (rest - middle.astype(F32)).astype(BF16)


def reverse_links(q, links):
    out = q & 1
    for i in range(links):
        out = out | (((q >> (1 + i)) & 1) << (links - i))
    return out


def other_core(j, links):
    return reverse_links(2 * j, links) | 1


def relative(place_ref, k, d):
    return lax.bitwise_xor(lax.bitwise_xor(lax.div(place_ref[0], k), place_ref[1]), d) * k


def label(place_ref, q, links):
    return jnp.where(lax.rem(place_ref[0], 2) == 1, reverse_links(q, links), q)


def tile_part(place_ref, k, s, tile):
    at = lax.bitwise_xor(lax.rem(place_ref[0], k), s)
    return pl.ds(pl.multiple_of(at * tile, LANES), tile)


def pack_kernel(place_ref, out_ref, gain_ref, weight_ref, *pieces):
    own, tile = out_ref.shape[0], pieces[0].shape[1]
    for s, piece in enumerate(pieces):
        part = tile_part(place_ref, len(pieces), s, tile)
        piece[0:own, :] = out_ref[:, part]
        if s == 0:
            head = gain_ref[:, part] * weight_ref[:, part]
            zero = jnp.zeros((1, tile), BF16)
            piece[own : own + 16, :] = jnp.concatenate([*split_three(head)] + [zero] * 13, axis=0)


def head_of(ref):
    wide = ref[...].astype(F32)
    return wide[0:1] + wide[1:2] + wide[2:3]


def turn(values):
    pad = jnp.zeros((LANES - values.shape[0], LANES), F32)
    return jnp.transpose(jnp.concatenate([values, pad], axis=0))


def sums_kernel(k, place_ref, head_ref, returns_ref, live_ref, *refs):
    pieces, sums_ref = refs[:-1], refs[-1]
    own = returns_ref.shape[1]
    head = head_of(head_ref)
    for d, piece in enumerate(pieces):
        at = relative(place_ref, k, d)
        for s in range(k):
            wide = piece[s].astype(F32)
            columns = place(
                [
                    jnp.sum(wide * wide, axis=1, keepdims=True),
                    jnp.sum(wide * head, axis=1, keepdims=True),
                ],
                own,
            )
            sums_ref[at + s] = turn(columns)[0:8]
    pad = jnp.zeros((1, LANES - own), F32)
    sublane = lax.broadcasted_iota(jnp.int32, (8, LANES), 0)
    targets = jnp.concatenate([returns_ref[...], pad], axis=1)
    live = jnp.concatenate([live_ref[...].astype(F32), pad], axis=1)
    mine = jnp.where(sublane == 2, targets, jnp.where(sublane == 3, live, 0.0))
    sums_ref[0] = sums_ref[0] + mine


def sum_rows_kernel(bit, sums_ref, came_ref, out_ref):
    for q in range(sums_ref.shape[0]):
        out_ref[q] = sums_ref[q] + came_ref[q ^ bit]


def gradient_rows(rows_of, token, head):
    root, dvalue, product = (column(token, i) for i in range(3))
    return (root * (head * dvalue - rows_of * root * product)).astype(BF16)


def out_kernel(width, k, bit, links, place_ref, head_ref, sums_ref, came_ref, *refs):
    pieces, (d_out_ref, token_ref, columns_ref) = refs[:-3], refs[-3:]
    rows, own = sums_ref.shape[0], d_out_ref.shape[1]
    head = head_of(head_ref)
    sums = [sums_ref[q] + came_ref[q ^ bit] for q in range(rows)]
    lives = functools.reduce(lambda a, b: a + b, [one[3:4] for one in sums])
    count = jnp.sum(lives, axis=1, keepdims=True)
    factor = (rows * own * math.sqrt(width)) / count
    for q, one in enumerate(sums):
        root = lax.rsqrt(one[0:1] / width + epsilon)
        value = root * one[1:2]
        dvalue = one[3:4] * (value - one[2:3]) * factor
        product = dvalue * value / width
        columns = jnp.concatenate([root, dvalue, product] + [jnp.zeros_like(root)] * 5, axis=0)
        columns_ref[q] = turn(columns)[0:own]
    token_ref[...] = columns_ref[0]
    for d, piece in enumerate(pieces):
        at = relative(place_ref, k, d)
        for s in range(k):
            d_out_ref[label(place_ref, at + s, links)] = gradient_rows(
                piece[s].astype(F32), columns_ref[at + s], head
            )


def partial_kernel(links, d_out_ref, w_ref, keep_ref, send_ref):
    count, own, tile = d_out_ref.shape
    result = lax.dot_general(
        d_out_ref[...].reshape(count * own, tile),
        w_ref[...],
        (((1,), (1,)), ((), ())),
        preferred_element_type=F32,
    ).astype(BF16)
    result = result.reshape(count, own, -1)
    for j in range(count // 2):
        keep_ref[j] = result[2 * j]
        send_ref[j] = result[other_core(j, links)]


def add_kernel(bit, keep_ref, came_ref, *outs):
    sent = kept = 0
    for q in range(keep_ref.shape[0]):
        total = (keep_ref[q].astype(F32) + came_ref[q].astype(F32)).astype(BF16)
        if len(outs) == 2 and q & bit:
            outs[1][sent] = total
            sent += 1
        else:
            outs[0][kept] = total
            kept += 1


def add(keep, came, bit, after=()):
    count, own, extent = keep.shape
    fb = block_of(extent, 2048 if count < 4 else 1024)
    block = pl.BlockSpec((count, own, fb), lambda i: (0, 0, i))
    parts = 2 if bit else 1
    out = pl.BlockSpec((count // parts, own, fb), lambda i: (0, 0, i))
    return call(
        functools.partial(add_kernel, bit),
        (extent // fb,),
        [block, block],
        [out] * parts,
        [jax.ShapeDtypeStruct((count // parts, own, extent), BF16)] * parts,
        [keep, came],
        cost=cost(count * own * extent, 6 * count * own * extent),
        after=after,
    )


def join_kernel(picks, *refs):
    for at, (i, j) in enumerate(picks):
        refs[-1][at] = refs[i][j]


def join(arrays, picks, after=()):
    own, extent = arrays[0].shape[1:]
    fb = block_of(extent, 1024)
    return call(
        functools.partial(join_kernel, picks),
        (extent // fb,),
        [pl.BlockSpec((array.shape[0], own, fb), lambda i: (0, 0, i)) for array in arrays],
        pl.BlockSpec((len(picks), own, fb), lambda i: (0, 0, i)),
        jax.ShapeDtypeStruct((len(picks), own, extent), BF16),
        arrays,
        cost=cost(0, 4 * len(picks) * own * extent),
        after=after,
    )


def every(*arrays):
    return [(i, j) for i, array in enumerate(arrays) for j in range(array.shape[0])]


def stack_kernel(count, *refs):
    for out in refs[count:]:
        for at in range(out.shape[0]):
            out[at] = refs[at][...]


def stack(arrays, own, counts):
    extent = arrays[0].shape[1]
    fb = block_of(extent, 2048)
    return call(
        functools.partial(stack_kernel, len(arrays)),
        (extent // fb,),
        [pl.BlockSpec((own, fb), lambda i: (0, i))] * len(arrays),
        [pl.BlockSpec((count, own, fb), lambda i: (0, 0, i)) for count in counts],
        [jax.ShapeDtypeStruct((count, own, extent), BF16) for count in counts],
        arrays,
        cost=cost(0, 4 * len(arrays) * own * extent),
    )


def weight_kernel(links, picks, held, d_out_ref, *refs):
    out_ref, done_ref = refs[-2:]
    mine, other = refs[:held], refs[held : 2 * held]
    count, own, tile = d_out_ref.shape
    hidden = [None] * count
    for j in range(count // 2):
        for pair, position in ((mine, 2 * j), (other, other_core(j, links))):
            gate, up = (pair[i][at].astype(F32) for i, at in picks[j])
            hidden[position] = (gate * jax.nn.sigmoid(gate) * up).astype(BF16)
    out_ref[...] = lax.dot_general(
        jnp.concatenate(hidden, axis=0),
        d_out_ref[...].reshape(count * own, tile),
        (((0,), (0,)), ((), ())),
        preferred_element_type=F32,
    )
    done_ref[...] = jnp.zeros_like(done_ref)


def normed_kernel(links, picks, held, first, last, k, place_ref, w_gate_ref, w_up_ref, *refs):
    out_ref, total = refs[-2:]
    mine, other = refs[:held], refs[held : 2 * held]
    mine_grad, other_grad = refs[2 * held : 2 * held + 2]
    before = None if first else refs[2 * held + 2]
    count, own = 2 * mine_grad.shape[0], mine_grad.shape[1]
    step = pl.program_id(0)

    d_gates, d_ups = [None] * count, [None] * count
    for j in range(count // 2):
        for pair, grad, position in (
            (mine, mine_grad, 2 * j),
            (other, other_grad, other_core(j, links)),
        ):
            gate, up = (pair[i][at].astype(F32) for i, at in picks[j])
            sig = jax.nn.sigmoid(gate)
            through = grad[j].astype(F32) * sig
            d_gates[position] = (through * up * (1.0 + gate * (1.0 - sig))).astype(BF16)
            d_ups[position] = (through * gate).astype(BF16)
    contracted = (((1,), (1,)), ((), ()))
    result = lax.dot_general(
        jnp.concatenate(d_gates, axis=0), w_gate_ref[...], contracted, preferred_element_type=F32
    ) + lax.dot_general(
        jnp.concatenate(d_ups, axis=0), w_up_ref[...], contracted, preferred_element_type=F32
    )

    @pl.when(step == 0)
    def _():
        total[...] = result if first else before[...] + result

    @pl.when(step > 0)
    def _():
        total[...] += result

    @pl.when(step == pl.num_programs(0) - 1)
    def _():
        if not last:
            out_ref[...] = total[...]
        else:
            for d in range(count // k):
                at = relative(place_ref, k, d)
                for s in range(k):
                    start = pl.multiple_of(label(place_ref, at + s, links) * own, 16)
                    out_ref[d * k + s] = total[pl.ds(start, own), :].astype(BF16)


def product_kernel(k, place_ref, mid_ref, gain_ref, *refs):
    backs, sums_ref = refs[:-1], refs[-1]
    own, tile = backs[0].shape
    products = squares = jnp.zeros((own, 1), F32)
    for s, back in enumerate(backs):
        part = tile_part(place_ref, k, s, tile)
        middle = mid_ref[:, part].astype(F32)
        products = products + jnp.sum(
            back[...].astype(F32) * gain_ref[:, part] * middle, axis=1, keepdims=True
        )
        squares = squares + jnp.sum(middle * middle, axis=1, keepdims=True)
    sums_ref[...] = place([products, squares], own)


def pair_kernel(first_ref, second_ref, out_ref):
    out_ref[...] = first_ref[...] + second_ref[...]


def result_kernel(width, k, place_ref, block_ref, mid_ref, norm_ref, weight_ref, gain_ref, token_ref, *refs):
    (sums_ref, came_ref), backs, out_ref = refs[:2], refs[2:-1], refs[-1]
    tile = backs[0].shape[1]
    sums = sums_ref[...] + came_ref[...]
    root = lax.rsqrt(column(sums, 1) / width + epsilon)
    product = column(sums, 0) * root / width
    for s, back in enumerate(backs):
        part = tile_part(place_ref, k, s, tile)
        own_d_out = gradient_rows(
            block_ref[:, part].astype(F32), token_ref[...], norm_ref[:, part] * weight_ref[:, part]
        )
        scaled = back[...].astype(F32) * gain_ref[:, part]
        normalized = mid_ref[:, part].astype(F32) * root
        out_ref[:, part] = (own_d_out.astype(F32) + root * (scaled - normalized * product)).astype(BF16)


def local(
    block_out,
    stream_mid,
    gate_pre,
    up_pre,
    final_gain,
    mlp_gain,
    value_weight,
    returns,
    response_mask,
    w_gate,
    w_up,
    w_down,
):
    rows, cols = lax.axis_size("row"), lax.axis_size("col")
    k = rows // cols
    own, block = block_out.shape
    width = block * cols
    tile = width // rows
    units = gate_pre.shape[1]
    ordered.clear()
    where = jnp.stack([lax.axis_index("row"), lax.axis_index("col")]).astype(jnp.int32)
    smem = pl.BlockSpec(memory_space=pltpu.SMEM)
    final_gain, mlp_gain, value_weight = final_gain[None, :], mlp_gain[None, :], value_weight[None, :]

    link_bits = bits_of(rows)[1:]
    links = len(link_bits)

    def across(values, bit):
        return lax.ppermute(values, "row", [(r, r ^ bit) for r in range(rows)])

    def linked(values, i):
        pairs = [(r, r ^ link_bits[links - 1 - i if r % 2 else i]) for r in range(rows)]
        return lax.ppermute(values, "row", pairs)

    def along(values, bit):
        return lax.ppermute(values, "col", [(c, c ^ bit) for c in range(cols)])

    def swap(values, s):
        pairs = [
            (r * cols + c, (k * c + ((r % k) ^ s)) * cols + r // k)
            for r in range(rows)
            for c in range(cols)
        ]
        return lax.ppermute(values, ("row", "col"), pairs)

    shapes = [(own + 16 * (s == 0), tile) for s in range(k)]
    packed = call(
        pack_kernel,
        (1,),
        [smem, whole((own, block)), whole((1, block)), whole((1, block))],
        [whole(shape) for shape in shapes],
        [jax.ShapeDtypeStruct(shape, BF16) for shape in shapes],
        [where, block_out, final_gain, value_weight],
        cost=cost(own * block, own * block * 4),
    )
    swapped = [swap(packed[s], s) for s in range(k)]

    (pieces,) = stack(swapped, own, [k])
    pieces = [pieces] + [along(pieces, d) for d in range(1, cols)]

    paired, gate_own = stack([gate_pre, up_pre], own, [2, 1])
    hop_a = linked(paired, 0)
    gate_b = linked(gate_own, 1)
    head_spec = pl.BlockSpec((16, tile), lambda i: (own // 16, 0))

    piece_specs = [whole((k, own, tile))] * cols
    sums = call(
        functools.partial(sums_kernel, k),
        (1,),
        [smem, head_spec, whole((1, own)), whole((1, own))] + piece_specs,
        whole((rows, 8, LANES)),
        jax.ShapeDtypeStruct((rows, 8, LANES), F32),
        [where, swapped[0], returns[None, :], response_mask[None, :], *pieces],
        cost=cost(rows * own * tile * 4, rows * own * tile * 2),
    )
    for bit in bits_of(rows)[:-1]:
        sums = call(
            functools.partial(sum_rows_kernel, bit),
            (1,),
            [whole((rows, 8, LANES))] * 2,
            whole((rows, 8, LANES)),
            jax.ShapeDtypeStruct((rows, 8, LANES), F32),
            [sums, across(sums, bit)],
            cost=cost(rows * 8 * LANES, rows * 8 * LANES * 12),
        )
    bit = bits_of(rows)[-1]
    d_out, token = call(
        functools.partial(out_kernel, width, k, bit, links),
        (1,),
        [smem, head_spec] + [whole((rows, 8, LANES))] * 2 + piece_specs,
        [whole((rows, own, tile)), whole((own, LANES))],
        [jax.ShapeDtypeStruct((rows, own, tile), BF16), jax.ShapeDtypeStruct((own, LANES), F32)],
        [where, swapped[0], sums, across(sums, bit), *pieces],
        scratch=[pltpu.VMEM((rows, own, LANES), F32)],
        cost=cost(rows * own * tile * 6, rows * own * tile * 4),
        after=[hop_a, gate_b],
    )

    paired, hop_a, gate_b, up_late, d_out = lax.optimization_barrier(
        (paired, hop_a, gate_b, up_pre[None], d_out)
    )
    up_b = linked(up_late, 1)
    held = [paired, hop_a, gate_b, up_b, linked(hop_a, 1)]
    picks = [((0, 0), (0, 1)), ((1, 0), (1, 1)), ((2, 0), (3, 0)), ((4, 0), (4, 1))]
    for i in range(2, links):
        picks = picks + [tuple((at + len(held), j) for at, j in pair) for pair in picks]
        held = held + [linked(values, i) for values in held]
    others = [across(values, 1) for values in held]

    lines = units // (2 * LANES)
    sizes = [lines // 3, lines // 3]
    sizes = [size * 2 * LANES for size in sizes + [lines - sum(sizes)]]
    chunks = [(sum(sizes[:i]), size) for i, size in enumerate(sizes)]
    count = rows // 2

    def reduced(number):
        start, extent = chunks[number]
        fb = block_of(math.gcd(start, extent), 1024)
        keep, send = call(
            functools.partial(partial_kernel, links),
            (extent // fb,),
            [
                whole((rows, own, tile)),
                pl.BlockSpec((fb, tile), lambda i, f=start // fb: (f + i, 0)),
            ],
            [pl.BlockSpec((count, own, fb), lambda i: (0, 0, i))] * 2,
            [jax.ShapeDtypeStruct((count, own, extent), BF16)] * 2,
            [d_out, w_down],
            limit=47,
            cost=cost(2 * rows * own * tile * extent, 2 * extent * tile + 2 * rows * own * extent),
            after=waits.get((number, 0), ()),
        )
        received = across(send, 1)
        yield
        for i in range(links):
            keep, send = add(keep, received, 1, waits.get((number, 1 + i), ()))
            received = linked(send, i)
            yield
        (keep,) = add(keep, received, 0, waits.get((number, links + 1), ()))
        for i in range(links):
            came = linked(keep, i)
            yield
            keep = join([keep, came], every(keep, came), waits.get((number, links + 2 + i), ()))
        grads[number] = (keep, across(keep, 1))
        yield

    def normed(number, total):
        start, extent = chunks[number]
        first, last = number == 0, number == len(chunks) - 1
        fb = block_of(math.gcd(start, extent), 1024)
        weights = pl.BlockSpec((tile, fb), lambda i, f=start // fb: (0, f + i))
        ins = (
            [smem, weights, weights]
            + [
                pl.BlockSpec((values.shape[0], own, fb), lambda i, f=start // fb: (0, 0, f + i))
                for values in held + others
            ]
            + [pl.BlockSpec((count, own, fb), lambda i: (0, 0, i))] * 2
        )
        args = [where, w_gate, w_up, *held, *others, *grads[number]]
        if not first:
            ins.append(whole((rows * own, tile)))
            args.append(total)
        shape = (rows, own, tile) if last else (rows * own, tile)
        return call(
            functools.partial(normed_kernel, links, picks, len(held), first, last, k),
            (extent // fb,),
            ins,
            whole(shape),
            jax.ShapeDtypeStruct(shape, BF16 if last else F32),
            args,
            scratch=[pltpu.VMEM((rows * own, tile), F32)],
            limit=36,
            cost=cost(
                4 * rows * own * tile * extent,
                4 * extent * tile + 6 * rows * own * extent,
                rows * own * extent,
            ),
        )

    waits = {
        (1, 0): others[:3],
        (2, 0): held[4:5],
        (1, links): others[4:5],
        (0, links + 1): [up_b],
        (0, links + 2): others[3:4],
    }
    grads, total = {}, None
    chains = [reduced(number) for number in range(len(chunks))]
    stages = 2 * links + 2
    for t in range(stages + len(chunks)):
        at = {number: t - number for number in range(len(chunks)) if 0 <= t - number <= stages}
        for number in sorted(at, key=lambda number: (at[number] == stages, -number)):
            if at[number] < stages:
                next(chains[number])
            else:
                total = normed(number, total)

    half = units // 2
    fb = block_of(half, 1024)
    blocks = half // fb
    d_w_down = None
    col_bits = bits_of(cols)
    for at, bit in enumerate(col_bits):
        n = total.shape[0] // (2 * k)
        split = total.reshape(n, 2, k, own, tile)
        keep, send = (split[:, side].reshape(n * k, own, tile) for side in range(2))
        received = along(send, bit)
        if at < 2:
            ins = [whole((rows, own, tile))] + [
                pl.BlockSpec((values.shape[0], own, fb), lambda i, at=at: (0, 0, at * blocks + i))
                for values in held + others
            ]
            args = [d_out, *held, *others]
            aliases = {}
            if at:
                ins.append(pl.BlockSpec(memory_space=pl.ANY))
                args.append(d_w_down)
                aliases = {len(args) - 1: 0}
            d_w_down, _ = call(
                functools.partial(weight_kernel, links, picks, len(held)),
                (blocks,),
                ins,
                [pl.BlockSpec((fb, tile), lambda i, at=at: (at * blocks + i, 0)), whole((8, LANES))],
                [jax.ShapeDtypeStruct((units, tile), F32), jax.ShapeDtypeStruct((8, LANES), F32)],
                args,
                cost=cost(
                    2 * rows * own * tile * half,
                    4 * half * tile + 4 * rows * own * half,
                    rows * own * half,
                ),
                aliases=aliases,
                limit=36,
            )
        (total,) = add(keep, received, 0)

    backs = [swap(total[s], s) for s in range(k)]
    row_spec, gain_spec = whole((own, block)), whole((1, block))
    sums_spec, back_specs = whole((own, LANES)), [whole((own, tile))] * k
    sums = call(
        functools.partial(product_kernel, k),
        (1,),
        [smem, row_spec, gain_spec] + back_specs,
        sums_spec,
        jax.ShapeDtypeStruct((own, LANES), F32),
        [where, stream_mid, mlp_gain, *backs],
        cost=cost(own * block * 5, own * block * 4),
    )
    for bit in col_bits[:-1]:
        sums = call(
            pair_kernel,
            (1,),
            [sums_spec] * 2,
            sums_spec,
            jax.ShapeDtypeStruct((own, LANES), F32),
            [sums, along(sums, bit)],
            cost=cost(own * LANES, own * LANES * 12),
        )
    gradient = call(
        functools.partial(result_kernel, width, k),
        (1,),
        [smem, row_spec, row_spec] + [gain_spec] * 3 + [sums_spec] * 3 + back_specs,
        row_spec,
        jax.ShapeDtypeStruct((own, block), BF16),
        [where, block_out, stream_mid, final_gain, value_weight, mlp_gain, token, sums]
        + [along(sums, col_bits[-1]), *backs],
        cost=cost(own * block * 14, own * block * 8),
    )
    return (gradient, d_w_down)


def solution(mesh):
    placed = (
        P("row", "col"),
        P("row", "col"),
        P("row", "col"),
        P("row", "col"),
        P("col"),
        P("col"),
        P("col"),
        P("row"),
        P("row"),
        P("row", "col"),
        P("row", "col"),
        P("col", "row"),
    )
    return jax.shard_map(
        local,
        mesh=mesh,
        in_specs=placed,
        out_specs=(P("row", "col"), P("col", "row")),
        check_vma=False,
    )
```

```python
import functools
import math

import jax
import jax.numpy as jnp
from jax import lax
from jax.experimental import pallas as pl
from jax.experimental.pallas import tpu as pltpu
from jax.sharding import PartitionSpec as P

epsilon = 1e-05
LANES = 128
MIB = 1024 * 1024
F32 = jnp.float32
BF16 = jnp.bfloat16


def bits_of(n):
    return [1 << i for i in range(n.bit_length() - 1)]


def block_of(extent, most):
    best = LANES
    for size in range(LANES, most + 1, LANES):
        if extent % size == 0:
            best = size
    return best


ordered = []


def call(kernel, grid, ins, outs, shapes, args, scratch=(), limit=32, cost=None, aliases={}, after=()):
    after = list(after) + ordered[-1:]
    known, extra = len(ins), len(after)

    def body(*refs):
        kernel(*refs[:known], *refs[known + extra :])

    result = pl.pallas_call(
        body,
        grid=grid,
        in_specs=list(ins) + [pl.BlockSpec(memory_space=pl.ANY)] * extra,
        out_specs=outs,
        out_shape=shapes,
        scratch_shapes=list(scratch),
        input_output_aliases=aliases,
        compiler_params=pltpu.CompilerParams(
            dimension_semantics=("arbitrary",) * len(grid), vmem_limit_bytes=limit * MIB
        ),
        cost_estimate=cost,
    )(*args, *after)
    ordered[:] = jax.tree.leaves(result)[-1:]
    return result


def cost(flops, moved, special=0):
    return pl.CostEstimate(flops=int(flops), bytes_accessed=int(moved), transcendentals=int(special))


def whole(shape):
    return pl.BlockSpec(shape, lambda i: (0,) * len(shape))


def column(values, position):
    return values[:, position : position + 1]


def place(columns, rows):
    lane = lax.broadcasted_iota(jnp.int32, (rows, LANES), 1)
    out = jnp.zeros((rows, LANES), F32)
    for position, values in enumerate(columns):
        out = jnp.where(lane == position, values, out)
    return out


def reverse_links(q, links):
    out = q & 1
    for i in range(links):
        out = out | (((q >> (1 + i)) & 1) << (links - i))
    return out


def other_core(j, links):
    return reverse_links(2 * j, links) | 1


def relative(place_ref, k, d):
    return lax.bitwise_xor(lax.bitwise_xor(lax.div(place_ref[0], k), place_ref[1]), d) * k


def label(place_ref, q, links):
    return jnp.where(lax.rem(place_ref[0], 2) == 1, reverse_links(q, links), q)


def slot(place_ref, k, links, d, s):
    own = lax.bitwise_xor(lax.rem(place_ref[0], k), s)
    return label(place_ref, relative(place_ref, k, d) + own, links)


def head_kernel(gain_ref, weight_ref, live_ref, head_ref, count_ref):
    head_ref[...] = gain_ref[...] * weight_ref[...]
    count = jnp.sum(live_ref[...].astype(F32), axis=1, keepdims=True)
    count_ref[...] = jnp.broadcast_to(count, count_ref.shape)


def turn(values):
    pad = jnp.zeros((LANES - values.shape[0], LANES), F32)
    return jnp.transpose(jnp.concatenate([values, pad], axis=0))


def gradient_rows(rows_of, token, head):
    root, dvalue, product = (column(token, i) for i in range(3))
    return (root * (head * dvalue - rows_of * root * product)).astype(BF16)


def out_kernel(tokens, k, links, place_ref, returns_ref, live_ref, count_ref, came_ref, *refs):
    columns = (len(refs) - 2) // (2 + k)
    pieces, heads, outs = refs[:columns], refs[columns : 2 * columns], refs[2 * columns : -2]
    token_ref, held_ref = refs[-2:]
    own, block = pieces[0].shape
    width, tile = block * columns, block // k
    squares = products = jnp.zeros((own, 1), F32)
    for piece, head in zip(pieces, heads):
        wide = piece[...].astype(F32)
        squares = squares + jnp.sum(wide * wide, axis=1, keepdims=True)
        products = products + jnp.sum(wide * head[...], axis=1, keepdims=True)
    pad = jnp.zeros((1, LANES - own), F32)
    rows = [returns_ref[...], live_ref[...].astype(F32)]
    rows = [jnp.concatenate([row, pad], axis=1) for row in rows] + [jnp.zeros((6, LANES), F32)]
    rows = turn(jnp.concatenate(rows, axis=0))[0:own]
    factor = (tokens * math.sqrt(width)) / (count_ref[0:1, 0:1] + came_ref[0:1, 0:1])
    root = lax.rsqrt(squares / width + epsilon)
    value = root * products
    dvalue = column(rows, 1) * (value - column(rows, 0)) * factor
    token = place([root, dvalue, dvalue * value / width], own)
    token_ref[...] = token
    for d in range(columns):
        for s in range(k):
            part = slice(s * tile, (s + 1) * tile)
            held_ref[slot(place_ref, k, links, d, s)] = gradient_rows(
                pieces[d][:, part].astype(F32), token, heads[d][:, part]
            )
    for q, out in enumerate(outs):
        out[...] = held_ref[q]


def arrange_kernel(k, links, place_ref, *refs):
    came, (keep_ref, send_ref, held_ref) = refs[:-3], refs[-3:]
    for q, ref in enumerate(came):
        held_ref[q] = ref[...]
    for d in range(len(came) // k):
        for s in range(k):
            (send_ref if d % 2 else keep_ref)[d // 2 * k + s] = held_ref[slot(place_ref, k, links, d, s)]


def partial_kernel(links, d_out_ref, w_ref, keep_ref, send_ref):
    count, own, tile = d_out_ref.shape
    result = lax.dot_general(
        d_out_ref[...].reshape(count * own, tile),
        w_ref[...],
        (((1,), (1,)), ((), ())),
        preferred_element_type=F32,
    ).astype(BF16)
    result = result.reshape(count, own, -1)
    for j in range(count // 2):
        keep_ref[j] = result[2 * j]
        send_ref[j] = result[other_core(j, links)]


def add_kernel(bit, keep_ref, came_ref, *outs):
    sent = kept = 0
    for q in range(keep_ref.shape[0]):
        total = (keep_ref[q].astype(F32) + came_ref[q].astype(F32)).astype(BF16)
        if len(outs) == 2 and q & bit:
            outs[1][sent] = total
            sent += 1
        else:
            outs[0][kept] = total
            kept += 1


def add(keep, came, bit, after=()):
    count, own, extent = keep.shape
    fb = block_of(extent, 2048 if count < 4 else 1024)
    block = pl.BlockSpec((count, own, fb), lambda i: (0, 0, i))
    parts = 2 if bit else 1
    out = pl.BlockSpec((count // parts, own, fb), lambda i: (0, 0, i))
    return call(
        functools.partial(add_kernel, bit),
        (extent // fb,),
        [block, block],
        [out] * parts,
        [jax.ShapeDtypeStruct((count // parts, own, extent), BF16)] * parts,
        [keep, came],
        cost=cost(count * own * extent, 6 * count * own * extent),
        after=after,
    )


def join_kernel(picks, *refs):
    for at, (i, j) in enumerate(picks):
        refs[-1][at] = refs[i][j]


def join(arrays, picks, after=()):
    own, extent = arrays[0].shape[1:]
    fb = block_of(extent, 1024)
    return call(
        functools.partial(join_kernel, picks),
        (extent // fb,),
        [pl.BlockSpec((array.shape[0], own, fb), lambda i: (0, 0, i)) for array in arrays],
        pl.BlockSpec((len(picks), own, fb), lambda i: (0, 0, i)),
        jax.ShapeDtypeStruct((len(picks), own, extent), BF16),
        arrays,
        cost=cost(0, 4 * len(picks) * own * extent),
        after=after,
    )


def every(*arrays):
    return [(i, j) for i, array in enumerate(arrays) for j in range(array.shape[0])]


def stack_kernel(count, *refs):
    for out in refs[count:]:
        for at in range(out.shape[0]):
            out[at] = refs[at][...]


def stack(arrays, own, counts, after=(), limit=32):
    extent = arrays[0].shape[1]
    fb = block_of(extent, 2048)
    return call(
        functools.partial(stack_kernel, len(arrays)),
        (extent // fb,),
        [pl.BlockSpec((own, fb), lambda i: (0, i))] * len(arrays),
        [pl.BlockSpec((count, own, fb), lambda i: (0, 0, i)) for count in counts],
        [jax.ShapeDtypeStruct((count, own, extent), BF16) for count in counts],
        arrays,
        cost=cost(0, 4 * len(arrays) * own * extent),
        after=after,
        limit=limit,
    )


def weight_kernel(links, picks, held, d_out_ref, *refs):
    out_ref, done_ref = refs[-2:]
    mine, other = refs[:held], refs[held : 2 * held]
    count, own, tile = d_out_ref.shape
    hidden = [None] * count
    for j in range(count // 2):
        for pair, position in ((mine, 2 * j), (other, other_core(j, links))):
            gate, up = (pair[i][at].astype(F32) for i, at in picks[j])
            hidden[position] = (gate * jax.nn.sigmoid(gate) * up).astype(BF16)
    out_ref[...] = lax.dot_general(
        jnp.concatenate(hidden, axis=0),
        d_out_ref[...].reshape(count * own, tile),
        (((0,), (0,)), ((), ())),
        preferred_element_type=F32,
    )
    done_ref[...] = jnp.zeros_like(done_ref)


def normed_kernel(links, picks, held, first, last, w_gate_ref, w_up_ref, *refs):
    total = refs[-1]
    outs = refs[2 * held + (2 if first else 3) : -1]
    mine, other = refs[:held], refs[held : 2 * held]
    mine_grad, other_grad = refs[2 * held : 2 * held + 2]
    before = None if first else refs[2 * held + 2]
    count, own = 2 * mine_grad.shape[0], mine_grad.shape[1]
    step = pl.program_id(0)

    d_gates, d_ups = [None] * count, [None] * count
    for j in range(count // 2):
        for pair, grad, position in (
            (mine, mine_grad, 2 * j),
            (other, other_grad, other_core(j, links)),
        ):
            gate, up = (pair[i][at].astype(F32) for i, at in picks[j])
            sig = jax.nn.sigmoid(gate)
            through = grad[j].astype(F32) * sig
            d_gates[position] = (through * up * (1.0 + gate * (1.0 - sig))).astype(BF16)
            d_ups[position] = (through * gate).astype(BF16)
    contracted = (((1,), (1,)), ((), ()))
    result = lax.dot_general(
        jnp.concatenate(d_gates, axis=0), w_gate_ref[...], contracted, preferred_element_type=F32
    ) + lax.dot_general(
        jnp.concatenate(d_ups, axis=0), w_up_ref[...], contracted, preferred_element_type=F32
    )

    @pl.when(step == 0)
    def _():
        total[...] = result if first else before[...] + result

    @pl.when(step > 0)
    def _():
        total[...] += result

    @pl.when(step == pl.num_programs(0) - 1)
    def _():
        if not last:
            outs[0][...] = total[...]
        else:
            for q, out in enumerate(outs):
                out[...] = total[q * own : (q + 1) * own, :].astype(BF16)


def product_kernel(mid_ref, gain_ref, back_ref, sums_ref):
    k, own, tile = back_ref.shape
    products = squares = jnp.zeros((own, 1), F32)
    for s in range(k):
        part = slice(s * tile, (s + 1) * tile)
        middle = mid_ref[:, part].astype(F32)
        products = products + jnp.sum(
            back_ref[s].astype(F32) * gain_ref[:, part] * middle, axis=1, keepdims=True
        )
        squares = squares + jnp.sum(middle * middle, axis=1, keepdims=True)
    sums_ref[...] = place([products, squares], own)


def pair_kernel(first_ref, second_ref, out_ref):
    out_ref[...] = first_ref[...] + second_ref[...]


def result_kernel(
    width, block_ref, mid_ref, head_ref, gain_ref, token_ref, sums_ref, came_ref, back_ref, out_ref
):
    k, own, tile = back_ref.shape
    sums = sums_ref[...] + came_ref[...]
    root = lax.rsqrt(column(sums, 1) / width + epsilon)
    product = column(sums, 0) * root / width
    for s in range(k):
        part = slice(s * tile, (s + 1) * tile)
        own_d_out = gradient_rows(block_ref[:, part].astype(F32), token_ref[...], head_ref[:, part])
        scaled = back_ref[s].astype(F32) * gain_ref[:, part]
        normalized = mid_ref[:, part].astype(F32) * root
        out_ref[:, part] = (own_d_out.astype(F32) + root * (scaled - normalized * product)).astype(BF16)


def local(
    block_out,
    stream_mid,
    gate_pre,
    up_pre,
    final_gain,
    mlp_gain,
    value_weight,
    returns,
    response_mask,
    w_gate,
    w_up,
    w_down,
):
    rows, cols = lax.axis_size("row"), lax.axis_size("col")
    k = rows // cols
    own, block = block_out.shape
    width = block * cols
    tile = width // rows
    units = gate_pre.shape[1]
    ordered.clear()
    where = jnp.stack([lax.axis_index("row"), lax.axis_index("col")]).astype(jnp.int32)
    smem = pl.BlockSpec(memory_space=pltpu.SMEM)
    final_gain, mlp_gain, value_weight = final_gain[None, :], mlp_gain[None, :], value_weight[None, :]

    link_bits = bits_of(rows)[1:]
    links = len(link_bits)

    def across(values, bit):
        return lax.ppermute(values, "row", [(r, r ^ bit) for r in range(rows)])

    def linked(values, i):
        pairs = [(r, r ^ link_bits[links - 1 - i if r % 2 else i]) for r in range(rows)]
        return lax.ppermute(values, "row", pairs)

    def along(values, bit):
        return lax.ppermute(values, "col", [(c, c ^ bit) for c in range(cols)])

    def exchanged(tiles):
        came = {0: tiles[0]}
        for q in range(1, rows):
            pairs = [(r, r ^ (reverse_links(q, links) if r % 2 else q)) for r in range(rows)]
            came[reverse_links(q, links) if q % 2 else q] = lax.ppermute(tiles[q], "row", pairs)
        return [came[q] for q in range(rows)]

    line = jax.ShapeDtypeStruct((8, LANES), F32)
    mask = response_mask[None, :]
    head, tally = call(
        head_kernel,
        (1,),
        [whole((1, block)), whole((1, block)), whole((1, own))],
        [whole((1, block)), whole((8, LANES))],
        [jax.ShapeDtypeStruct((1, block), F32), line],
        [final_gain, value_weight, mask],
        cost=cost(block, block * 12),
    )
    heads = [head] + [along(head, d) for d in range(1, cols)]
    pieces = [block_out] + [along(block_out, d) for d in range(1, cols)]
    for bit in link_bits:
        tally = call(
            pair_kernel,
            (1,),
            [whole((8, LANES))] * 2,
            whole((8, LANES)),
            line,
            [tally, across(tally, bit)],
            cost=cost(8 * LANES, 8 * LANES * 12),
        )

    paired, gate_own = stack([gate_pre, up_pre], own, [2, 1], after=heads[1:], limit=60)
    hop_a = linked(paired, 0)
    gate_b = linked(gate_own, 1)

    *tiles, token = call(
        functools.partial(out_kernel, own * rows, k, links),
        (1,),
        [smem, whole((1, own)), whole((1, own)), whole((8, LANES)), whole((8, LANES))]
        + [whole((own, block))] * cols
        + [whole((1, block))] * cols,
        [whole((own, tile))] * rows + [whole((own, LANES))],
        [jax.ShapeDtypeStruct((own, tile), BF16)] * rows + [jax.ShapeDtypeStruct((own, LANES), F32)],
        [where, returns[None, :], mask, tally, across(tally, 1), *pieces, *heads],
        scratch=[pltpu.VMEM((rows, own, tile), BF16)],
        cost=cost(own * width * 10, own * width * 4),
    )
    (d_out,) = stack(exchanged(tiles), own, [rows], after=[hop_a, gate_b])

    paired, hop_a, gate_b, up_late, d_out = lax.optimization_barrier(
        (paired, hop_a, gate_b, up_pre[None], d_out)
    )
    up_b = linked(up_late, 1)
    held = [paired, hop_a, gate_b, up_b, linked(hop_a, 1)]
    picks = [((0, 0), (0, 1)), ((1, 0), (1, 1)), ((2, 0), (3, 0)), ((4, 0), (4, 1))]
    for i in range(2, links):
        picks = picks + [tuple((at + len(held), j) for at, j in pair) for pair in picks]
        held = held + [linked(values, i) for values in held]
    others = [across(values, 1) for values in held]

    lines = units // (2 * LANES)
    sizes = [lines // 3, lines // 3]
    sizes = [size * 2 * LANES for size in sizes + [lines - sum(sizes)]]
    chunks = [(sum(sizes[:i]), size) for i, size in enumerate(sizes)]
    count = rows // 2

    def reduced(number):
        start, extent = chunks[number]
        fb = block_of(math.gcd(start, extent), 1024)
        keep, send = call(
            functools.partial(partial_kernel, links),
            (extent // fb,),
            [
                whole((rows, own, tile)),
                pl.BlockSpec((fb, tile), lambda i, f=start // fb: (f + i, 0)),
            ],
            [pl.BlockSpec((count, own, fb), lambda i: (0, 0, i))] * 2,
            [jax.ShapeDtypeStruct((count, own, extent), BF16)] * 2,
            [d_out, w_down],
            limit=47,
            cost=cost(2 * rows * own * tile * extent, 2 * extent * tile + 2 * rows * own * extent),
            after=waits.get((number, 0), ()),
        )
        received = across(send, 1)
        yield
        for i in range(links):
            keep, send = add(keep, received, 1, waits.get((number, 1 + i), ()))
            received = linked(send, i)
            yield
        (keep,) = add(keep, received, 0, waits.get((number, links + 1), ()))
        for i in range(links):
            came = linked(keep, i)
            yield
            keep = join([keep, came], every(keep, came), waits.get((number, links + 2 + i), ()))
        grads[number] = (keep, across(keep, 1))
        yield

    def normed(number, total):
        start, extent = chunks[number]
        first, last = number == 0, number == len(chunks) - 1
        fb = block_of(math.gcd(start, extent), 1024)
        weights = pl.BlockSpec((tile, fb), lambda i, f=start // fb: (0, f + i))
        ins = (
            [weights, weights]
            + [
                pl.BlockSpec((values.shape[0], own, fb), lambda i, f=start // fb: (0, 0, f + i))
                for values in held + others
            ]
            + [pl.BlockSpec((count, own, fb), lambda i: (0, 0, i))] * 2
        )
        args = [w_gate, w_up, *held, *others, *grads[number]]
        if not first:
            ins.append(whole((rows * own, tile)))
            args.append(total)
        shape, kind, parts = ((own, tile), BF16, rows) if last else ((rows * own, tile), F32, 1)
        result = call(
            functools.partial(normed_kernel, links, picks, len(held), first, last),
            (extent // fb,),
            ins,
            [whole(shape)] * parts,
            [jax.ShapeDtypeStruct(shape, kind)] * parts,
            args,
            scratch=[pltpu.VMEM((rows * own, tile), F32)],
            limit=36,
            cost=cost(
                4 * rows * own * tile * extent,
                4 * extent * tile + 6 * rows * own * extent,
                rows * own * extent,
            ),
        )
        return result if last else result[0]

    waits = {
        (1, 0): others[:3],
        (2, 0): held[3:5],
        (1, links): others[4:5],
        (0, links + 2): others[3:4],
    }
    grads, total = {}, None
    chains = [reduced(number) for number in range(len(chunks))]
    stages = 2 * links + 2
    for t in range(stages + len(chunks)):
        at = {number: t - number for number in range(len(chunks)) if 0 <= t - number <= stages}
        for number in sorted(at, key=lambda number: (at[number] == stages, -number)):
            if at[number] < stages:
                next(chains[number])
            else:
                total = normed(number, total)

    keep, send = call(
        functools.partial(arrange_kernel, k, links),
        (1,),
        [smem] + [whole((own, tile))] * rows,
        [whole((count, own, tile))] * 2,
        [jax.ShapeDtypeStruct((count, own, tile), BF16)] * 2,
        [where, *exchanged(total)],
        scratch=[pltpu.VMEM((rows, own, tile), BF16)],
        cost=cost(0, rows * own * tile * 4),
    )
    half = units // 2
    fb = block_of(half, 1024)
    blocks = half // fb
    d_w_down = None
    col_bits = bits_of(cols)
    for at, bit in enumerate(col_bits):
        received = along(send, bit)
        if at < 2:
            ins = [whole((rows, own, tile))] + [
                pl.BlockSpec((values.shape[0], own, fb), lambda i, at=at: (0, 0, at * blocks + i))
                for values in held + others
            ]
            args = [d_out, *held, *others]
            aliases = {}
            if at:
                ins.append(pl.BlockSpec(memory_space=pl.ANY))
                args.append(d_w_down)
                aliases = {len(args) - 1: 0}
            d_w_down, _ = call(
                functools.partial(weight_kernel, links, picks, len(held)),
                (blocks,),
                ins,
                [pl.BlockSpec((fb, tile), lambda i, at=at: (at * blocks + i, 0)), whole((8, LANES))],
                [jax.ShapeDtypeStruct((units, tile), F32), jax.ShapeDtypeStruct((8, LANES), F32)],
                args,
                cost=cost(
                    2 * rows * own * tile * half,
                    4 * half * tile + 4 * rows * own * half,
                    rows * own * half,
                ),
                aliases=aliases,
                limit=36,
            )
        if bit == col_bits[-1]:
            (total,) = add(keep, received, 0)
        else:
            keep, send = add(keep, received, k)

    row_spec, gain_spec = whole((own, block)), whole((1, block))
    sums_spec, back_spec = whole((own, LANES)), whole((k, own, tile))
    sums = call(
        product_kernel,
        (1,),
        [row_spec, gain_spec, back_spec],
        sums_spec,
        jax.ShapeDtypeStruct((own, LANES), F32),
        [stream_mid, mlp_gain, total],
        cost=cost(own * block * 5, own * block * 4),
    )
    for bit in col_bits[:-1]:
        sums = call(
            pair_kernel,
            (1,),
            [sums_spec] * 2,
            sums_spec,
            jax.ShapeDtypeStruct((own, LANES), F32),
            [sums, along(sums, bit)],
            cost=cost(own * LANES, own * LANES * 12),
        )
    gradient = call(
        functools.partial(result_kernel, width),
        (1,),
        [row_spec, row_spec, gain_spec, gain_spec] + [sums_spec] * 3 + [back_spec],
        row_spec,
        jax.ShapeDtypeStruct((own, block), BF16),
        [block_out, stream_mid, head, mlp_gain, token, sums, along(sums, col_bits[-1]), total],
        cost=cost(own * block * 14, own * block * 8),
    )
    return (gradient, d_w_down)


def solution(mesh):
    placed = (
        P("row", "col"),
        P("row", "col"),
        P("row", "col"),
        P("row", "col"),
        P("col"),
        P("col"),
        P("col"),
        P("row"),
        P("row"),
        P("row", "col"),
        P("row", "col"),
        P("col", "row"),
    )
    return jax.shard_map(
        local,
        mesh=mesh,
        in_specs=placed,
        out_specs=(P("row", "col"), P("col", "row")),
        check_vma=False,
    )
```

```python
import functools
import math

import jax
import jax.numpy as jnp
from jax import lax
from jax.experimental import pallas as pl
from jax.experimental.pallas import tpu as pltpu
from jax.sharding import PartitionSpec as P

epsilon = 1e-05
LANES = 128
MIB = 1024 * 1024
F32 = jnp.float32
BF16 = jnp.bfloat16


def bits_of(n):
    return [1 << i for i in range(n.bit_length() - 1)]


def block_of(extent, most):
    best = LANES
    for size in range(LANES, most + 1, LANES):
        if extent % size == 0:
            best = size
    return best


ordered = []


def call(kernel, grid, ins, outs, shapes, args, scratch=(), limit=32, cost=None, aliases={}, after=()):
    after = list(after) + ordered[-1:]
    known, extra = len(ins), len(after)

    def body(*refs):
        kernel(*refs[:known], *refs[known + extra :])

    result = pl.pallas_call(
        body,
        grid=grid,
        in_specs=list(ins) + [pl.BlockSpec(memory_space=pl.ANY)] * extra,
        out_specs=outs,
        out_shape=shapes,
        scratch_shapes=list(scratch),
        input_output_aliases=aliases,
        compiler_params=pltpu.CompilerParams(
            dimension_semantics=("arbitrary",) * len(grid), vmem_limit_bytes=limit * MIB
        ),
        cost_estimate=cost,
    )(*args, *after)
    ordered[:] = jax.tree.leaves(result)[-1:]
    return result


def cost(flops, moved, special=0):
    return pl.CostEstimate(flops=int(flops), bytes_accessed=int(moved), transcendentals=int(special))


def whole(shape):
    return pl.BlockSpec(shape, lambda i: (0,) * len(shape))


def column(values, position):
    return values[:, position : position + 1]


def place(columns, rows):
    lane = lax.broadcasted_iota(jnp.int32, (rows, LANES), 1)
    out = jnp.zeros((rows, LANES), F32)
    for position, values in enumerate(columns):
        out = jnp.where(lane == position, values, out)
    return out


def reverse_links(q, links):
    out = q & 1
    for i in range(links):
        out = out | (((q >> (1 + i)) & 1) << (links - i))
    return out


def other_core(j, links):
    return reverse_links(2 * j, links) | 1


def relative(place_ref, k, d):
    return lax.bitwise_xor(lax.bitwise_xor(lax.div(place_ref[0], k), place_ref[1]), d) * k


def label(place_ref, q, links):
    return jnp.where(lax.rem(place_ref[0], 2) == 1, reverse_links(q, links), q)


def slot(place_ref, k, links, d, s):
    own = lax.bitwise_xor(lax.rem(place_ref[0], k), s)
    return label(place_ref, relative(place_ref, k, d) + own, links)


def head_kernel(gain_ref, weight_ref, head_ref):
    head_ref[...] = gain_ref[...] * weight_ref[...]


def turn(values):
    pad = jnp.zeros((LANES - values.shape[0], LANES), F32)
    return jnp.transpose(jnp.concatenate([values, pad], axis=0))


def gradient_rows(rows_of, token, head):
    root, dvalue, product = (column(token, i) for i in range(3))
    return (root * (head * dvalue - rows_of * root * product)).astype(BF16)


def out_kernel(tokens, k, links, place_ref, returns_ref, live_ref, *refs):
    columns = (len(refs) - 2) // (2 + k)
    pieces, heads, outs = refs[:columns], refs[columns : 2 * columns], refs[2 * columns : -2]
    token_ref, held_ref = refs[-2:]
    own, block = pieces[0].shape
    width, tile = block * columns, block // k
    squares = products = jnp.zeros((own, 1), F32)
    for piece, head in zip(pieces, heads):
        wide = piece[...].astype(F32)
        squares = squares + jnp.sum(wide * wide, axis=1, keepdims=True)
        products = products + jnp.sum(wide * head[...], axis=1, keepdims=True)
    pad = jnp.zeros((1, LANES - own), F32)
    rows = [returns_ref[...], live_ref[...].astype(F32)]
    rows = [jnp.concatenate([row, pad], axis=1) for row in rows] + [jnp.zeros((6, LANES), F32)]
    rows = turn(jnp.concatenate(rows, axis=0))[0:own]
    factor = tokens * math.sqrt(width)
    count = jnp.sum(column(rows, 1), axis=0, keepdims=True)
    root = lax.rsqrt(squares / width + epsilon)
    value = root * products
    dvalue = column(rows, 1) * (value - column(rows, 0)) * factor
    token = place([root, dvalue, dvalue * value / width], own)
    token_ref[...] = token
    for d in range(columns):
        for s in range(k):
            part = slice(s * tile, (s + 1) * tile)
            held_ref[slot(place_ref, k, links, d, s)] = gradient_rows(
                pieces[d][:, part].astype(F32), token, heads[d][:, part]
            )
    for q, out in enumerate(outs):
        out[0:own, :] = held_ref[q]
        out[own:, :] = jnp.broadcast_to(count, (out.shape[0] - own, tile)).astype(BF16)


def gather_kernel(*refs):
    tiles, (out_ref, inverse_ref) = refs[:-2], refs[-2:]
    own = out_ref.shape[1]
    count = 0.0
    for q, ref in enumerate(tiles):
        out_ref[q] = ref[0:own, :]
        count = count + ref[own : own + 16, 0:LANES].astype(F32)
    inverse_ref[...] = 1.0 / count[0:8]


def arrange_kernel(k, links, place_ref, *refs):
    came, (keep_ref, send_ref, held_ref) = refs[:-3], refs[-3:]
    for q, ref in enumerate(came):
        held_ref[q] = ref[...]
    for d in range(len(came) // k):
        for s in range(k):
            (send_ref if d % 2 else keep_ref)[d // 2 * k + s] = held_ref[slot(place_ref, k, links, d, s)]


def partial_kernel(links, d_out_ref, w_ref, keep_ref, send_ref):
    count, own, tile = d_out_ref.shape
    result = lax.dot_general(
        d_out_ref[...].reshape(count * own, tile),
        w_ref[...],
        (((1,), (1,)), ((), ())),
        preferred_element_type=F32,
    ).astype(BF16)
    result = result.reshape(count, own, -1)
    for j in range(count // 2):
        keep_ref[j] = result[2 * j]
        send_ref[j] = result[other_core(j, links)]


def add_kernel(bit, keep_ref, came_ref, *outs):
    sent = kept = 0
    for q in range(keep_ref.shape[0]):
        total = (keep_ref[q].astype(F32) + came_ref[q].astype(F32)).astype(BF16)
        if len(outs) == 2 and q & bit:
            outs[1][sent] = total
            sent += 1
        else:
            outs[0][kept] = total
            kept += 1


def add(keep, came, bit, after=()):
    count, own, extent = keep.shape
    fb = block_of(extent, 2048 if count < 4 else 1024)
    block = pl.BlockSpec((count, own, fb), lambda i: (0, 0, i))
    parts = 2 if bit else 1
    out = pl.BlockSpec((count // parts, own, fb), lambda i: (0, 0, i))
    return call(
        functools.partial(add_kernel, bit),
        (extent // fb,),
        [block, block],
        [out] * parts,
        [jax.ShapeDtypeStruct((count // parts, own, extent), BF16)] * parts,
        [keep, came],
        cost=cost(count * own * extent, 6 * count * own * extent),
        after=after,
    )


def join_kernel(picks, *refs):
    for at, (i, j) in enumerate(picks):
        refs[-1][at] = refs[i][j]


def join(arrays, picks, after=()):
    own, extent = arrays[0].shape[1:]
    fb = block_of(extent, 1024)
    return call(
        functools.partial(join_kernel, picks),
        (extent // fb,),
        [pl.BlockSpec((array.shape[0], own, fb), lambda i: (0, 0, i)) for array in arrays],
        pl.BlockSpec((len(picks), own, fb), lambda i: (0, 0, i)),
        jax.ShapeDtypeStruct((len(picks), own, extent), BF16),
        arrays,
        cost=cost(0, 4 * len(picks) * own * extent),
        after=after,
    )


def every(*arrays):
    return [(i, j) for i, array in enumerate(arrays) for j in range(array.shape[0])]


def stack_kernel(count, *refs):
    for out in refs[count:]:
        for at in range(out.shape[0]):
            out[at] = refs[at][...]


def stack(arrays, own, counts, after=(), limit=32):
    extent = arrays[0].shape[1]
    fb = block_of(extent, 2048)
    return call(
        functools.partial(stack_kernel, len(arrays)),
        (extent // fb,),
        [pl.BlockSpec((own, fb), lambda i: (0, i))] * len(arrays),
        [pl.BlockSpec((count, own, fb), lambda i: (0, 0, i)) for count in counts],
        [jax.ShapeDtypeStruct((count, own, extent), BF16) for count in counts],
        arrays,
        cost=cost(0, 4 * len(arrays) * own * extent),
        after=after,
        limit=limit,
    )


def weight_kernel(links, picks, held, inverse_ref, d_out_ref, *refs):
    out_ref, done_ref = refs[-2:]
    mine, other = refs[:held], refs[held : 2 * held]
    count, own, tile = d_out_ref.shape
    hidden = [None] * count
    for j in range(count // 2):
        for pair, position in ((mine, 2 * j), (other, other_core(j, links))):
            gate, up = (pair[i][at].astype(F32) for i, at in picks[j])
            hidden[position] = (gate * jax.nn.sigmoid(gate) * up).astype(BF16)
    out_ref[...] = inverse_ref[0:1, 0:1] * lax.dot_general(
        jnp.concatenate(hidden, axis=0),
        d_out_ref[...].reshape(count * own, tile),
        (((0,), (0,)), ((), ())),
        preferred_element_type=F32,
    )
    done_ref[...] = jnp.zeros_like(done_ref)


def normed_kernel(links, picks, held, first, last, inverse_ref, w_gate_ref, w_up_ref, *refs):
    total = refs[-1]
    outs = refs[2 * held + (2 if first else 3) : -1]
    mine, other = refs[:held], refs[held : 2 * held]
    mine_grad, other_grad = refs[2 * held : 2 * held + 2]
    before = None if first else refs[2 * held + 2]
    count, own = 2 * mine_grad.shape[0], mine_grad.shape[1]
    step = pl.program_id(0)

    d_gates, d_ups = [None] * count, [None] * count
    for j in range(count // 2):
        for pair, grad, position in (
            (mine, mine_grad, 2 * j),
            (other, other_grad, other_core(j, links)),
        ):
            gate, up = (pair[i][at].astype(F32) for i, at in picks[j])
            sig = jax.nn.sigmoid(gate)
            through = grad[j].astype(F32) * inverse_ref[0:1, 0:1] * sig
            d_gates[position] = (through * up * (1.0 + gate * (1.0 - sig))).astype(BF16)
            d_ups[position] = (through * gate).astype(BF16)
    contracted = (((1,), (1,)), ((), ()))
    result = lax.dot_general(
        jnp.concatenate(d_gates, axis=0), w_gate_ref[...], contracted, preferred_element_type=F32
    ) + lax.dot_general(
        jnp.concatenate(d_ups, axis=0), w_up_ref[...], contracted, preferred_element_type=F32
    )

    @pl.when(step == 0)
    def _():
        total[...] = result if first else before[...] + result

    @pl.when(step > 0)
    def _():
        total[...] += result

    @pl.when(step == pl.num_programs(0) - 1)
    def _():
        if not last:
            outs[0][...] = total[...]
        else:
            for q, out in enumerate(outs):
                out[...] = total[q * own : (q + 1) * own, :].astype(BF16)


def product_kernel(mid_ref, gain_ref, back_ref, sums_ref):
    k, own, tile = back_ref.shape
    products = squares = jnp.zeros((own, 1), F32)
    for s in range(k):
        part = slice(s * tile, (s + 1) * tile)
        middle = mid_ref[:, part].astype(F32)
        products = products + jnp.sum(
            back_ref[s].astype(F32) * gain_ref[:, part] * middle, axis=1, keepdims=True
        )
        squares = squares + jnp.sum(middle * middle, axis=1, keepdims=True)
    sums_ref[...] = place([products, squares], own)


def pair_kernel(first_ref, second_ref, out_ref):
    out_ref[...] = first_ref[...] + second_ref[...]


def result_kernel(
    width, block_ref, mid_ref, head_ref, gain_ref, inverse_ref, token_ref, sums_ref, came_ref, back_ref, out_ref
):
    k, own, tile = back_ref.shape
    sums = sums_ref[...] + came_ref[...]
    root = lax.rsqrt(column(sums, 1) / width + epsilon)
    product = column(sums, 0) * root / width
    inverse = inverse_ref[0:1, 0:1]
    token = place([column(token_ref, 0), column(token_ref, 1) * inverse, column(token_ref, 2) * inverse], own)
    for s in range(k):
        part = slice(s * tile, (s + 1) * tile)
        own_d_out = gradient_rows(block_ref[:, part].astype(F32), token, head_ref[:, part])
        scaled = back_ref[s].astype(F32) * gain_ref[:, part]
        normalized = mid_ref[:, part].astype(F32) * root
        out_ref[:, part] = (own_d_out.astype(F32) + root * (scaled - normalized * product)).astype(BF16)


def local(
    block_out,
    stream_mid,
    gate_pre,
    up_pre,
    final_gain,
    mlp_gain,
    value_weight,
    returns,
    response_mask,
    w_gate,
    w_up,
    w_down,
):
    rows, cols = lax.axis_size("row"), lax.axis_size("col")
    k = rows // cols
    own, block = block_out.shape
    width = block * cols
    tile = width // rows
    units = gate_pre.shape[1]
    ordered.clear()
    where = jnp.stack([lax.axis_index("row"), lax.axis_index("col")]).astype(jnp.int32)
    smem = pl.BlockSpec(memory_space=pltpu.SMEM)
    final_gain, mlp_gain, value_weight = final_gain[None, :], mlp_gain[None, :], value_weight[None, :]

    link_bits = bits_of(rows)[1:]
    links = len(link_bits)

    def across(values, bit):
        return lax.ppermute(values, "row", [(r, r ^ bit) for r in range(rows)])

    def linked(values, i):
        pairs = [(r, r ^ link_bits[links - 1 - i if r % 2 else i]) for r in range(rows)]
        return lax.ppermute(values, "row", pairs)

    def along(values, bit):
        return lax.ppermute(values, "col", [(c, c ^ bit) for c in range(cols)])

    def exchanged(tiles):
        came = {0: tiles[0]}
        for q in range(1, rows):
            pairs = [(r, r ^ (reverse_links(q, links) if r % 2 else q)) for r in range(rows)]
            came[reverse_links(q, links) if q % 2 else q] = lax.ppermute(tiles[q], "row", pairs)
        return [came[q] for q in range(rows)]

    line = jax.ShapeDtypeStruct((8, LANES), F32)
    head = call(
        head_kernel,
        (1,),
        [whole((1, block)), whole((1, block))],
        whole((1, block)),
        jax.ShapeDtypeStruct((1, block), F32),
        [final_gain, value_weight],
        cost=cost(block, block * 12),
        limit=60,
    )
    heads = [head] + [along(head, d) for d in range(1, cols)]
    pieces = [block_out] + [along(block_out, d) for d in range(1, cols)]

    paired, gate_own = stack([gate_pre, up_pre], own, [2, 1], after=heads[1:])
    hop_a = linked(paired, 0)
    gate_b = linked(gate_own, 1)

    *tiles, token = call(
        functools.partial(out_kernel, own * rows, k, links),
        (1,),
        [smem, whole((1, own)), whole((1, own))]
        + [whole((own, block))] * cols
        + [whole((1, block))] * cols,
        [whole((own + 16, tile))] * rows + [whole((own, LANES))],
        [jax.ShapeDtypeStruct((own + 16, tile), BF16)] * rows + [jax.ShapeDtypeStruct((own, LANES), F32)],
        [where, returns[None, :], response_mask[None, :], *pieces, *heads],
        scratch=[pltpu.VMEM((rows, own, tile), BF16)],
        cost=cost(own * width * 10, own * width * 4),
    )
    d_out, inverse = call(
        gather_kernel,
        (1,),
        [whole((own + 16, tile))] * rows,
        [whole((rows, own, tile)), whole((8, LANES))],
        [jax.ShapeDtypeStruct((rows, own, tile), BF16), line],
        exchanged(tiles),
        cost=cost(0, rows * own * tile * 4),
        after=[hop_a, gate_b],
    )

    paired, hop_a, gate_b, up_late, d_out = lax.optimization_barrier(
        (paired, hop_a, gate_b, up_pre[None], d_out)
    )
    up_b = linked(up_late, 1)
    held = [paired, hop_a, gate_b, up_b, linked(hop_a, 1)]
    picks = [((0, 0), (0, 1)), ((1, 0), (1, 1)), ((2, 0), (3, 0)), ((4, 0), (4, 1))]
    for i in range(2, links):
        picks = picks + [tuple((at + len(held), j) for at, j in pair) for pair in picks]
        held = held + [linked(values, i) for values in held]
    others = [across(values, 1) for values in held]

    lines = units // (2 * LANES)
    sizes = [lines // 3, lines // 3]
    sizes = [size * 2 * LANES for size in sizes + [lines - sum(sizes)]]
    chunks = [(sum(sizes[:i]), size) for i, size in enumerate(sizes)]
    count = rows // 2

    def reduced(number):
        start, extent = chunks[number]
        fb = block_of(math.gcd(start, extent), 1024)
        keep, send = call(
            functools.partial(partial_kernel, links),
            (extent // fb,),
            [
                whole((rows, own, tile)),
                pl.BlockSpec((fb, tile), lambda i, f=start // fb: (f + i, 0)),
            ],
            [pl.BlockSpec((count, own, fb), lambda i: (0, 0, i))] * 2,
            [jax.ShapeDtypeStruct((count, own, extent), BF16)] * 2,
            [d_out, w_down],
            limit=47,
            cost=cost(2 * rows * own * tile * extent, 2 * extent * tile + 2 * rows * own * extent),
            after=waits.get((number, 0), ()),
        )
        received = across(send, 1)
        yield
        for i in range(links):
            keep, send = add(keep, received, 1, waits.get((number, 1 + i), ()))
            received = linked(send, i)
            yield
        (keep,) = add(keep, received, 0, waits.get((number, links + 1), ()))
        for i in range(links):
            came = linked(keep, i)
            yield
            keep = join([keep, came], every(keep, came), waits.get((number, links + 2 + i), ()))
        grads[number] = (keep, across(keep, 1))
        yield

    def normed(number, total):
        start, extent = chunks[number]
        first, last = number == 0, number == len(chunks) - 1
        fb = block_of(math.gcd(start, extent), 1024)
        weights = pl.BlockSpec((tile, fb), lambda i, f=start // fb: (0, f + i))
        ins = (
            [whole((8, LANES)), weights, weights]
            + [
                pl.BlockSpec((values.shape[0], own, fb), lambda i, f=start // fb: (0, 0, f + i))
                for values in held + others
            ]
            + [pl.BlockSpec((count, own, fb), lambda i: (0, 0, i))] * 2
        )
        args = [inverse, w_gate, w_up, *held, *others, *grads[number]]
        if not first:
            ins.append(whole((rows * own, tile)))
            args.append(total)
        shape, kind, parts = ((own, tile), BF16, rows) if last else ((rows * own, tile), F32, 1)
        result = call(
            functools.partial(normed_kernel, links, picks, len(held), first, last),
            (extent // fb,),
            ins,
            [whole(shape)] * parts,
            [jax.ShapeDtypeStruct(shape, kind)] * parts,
            args,
            scratch=[pltpu.VMEM((rows * own, tile), F32)],
            limit=36,
            cost=cost(
                4 * rows * own * tile * extent,
                4 * extent * tile + 6 * rows * own * extent,
                rows * own * extent,
            ),
        )
        return result if last else result[0]

    waits = {
        (1, 0): others[:3],
        (1, 1): held[3:5],
        (1, links): others[4:5],
        (0, links + 2): others[3:4],
    }
    grads, total = {}, None
    chains = [reduced(number) for number in range(len(chunks))]
    stages = 2 * links + 2
    for t in range(stages + len(chunks)):
        at = {number: t - number for number in range(len(chunks)) if 0 <= t - number <= stages}
        for number in sorted(at, key=lambda number: ((at[number] == stages) == (t > stages), -number)):
            if at[number] < stages:
                next(chains[number])
            else:
                total = normed(number, total)

    keep, send = call(
        functools.partial(arrange_kernel, k, links),
        (1,),
        [smem] + [whole((own, tile))] * rows,
        [whole((count, own, tile))] * 2,
        [jax.ShapeDtypeStruct((count, own, tile), BF16)] * 2,
        [where, *exchanged(total)],
        scratch=[pltpu.VMEM((rows, own, tile), BF16)],
        cost=cost(0, rows * own * tile * 4),
    )
    half = units // 2
    fb = block_of(half, 1024)
    blocks = half // fb
    d_w_down = None
    col_bits = bits_of(cols)
    for at, bit in enumerate(col_bits):
        received = along(send, bit)
        if at < 2:
            ins = [whole((8, LANES)), whole((rows, own, tile))] + [
                pl.BlockSpec((values.shape[0], own, fb), lambda i, at=at: (0, 0, at * blocks + i))
                for values in held + others
            ]
            args = [inverse, d_out, *held, *others]
            aliases = {}
            if at:
                ins.append(pl.BlockSpec(memory_space=pl.ANY))
                args.append(d_w_down)
                aliases = {len(args) - 1: 0}
            d_w_down, _ = call(
                functools.partial(weight_kernel, links, picks, len(held)),
                (blocks,),
                ins,
                [pl.BlockSpec((fb, tile), lambda i, at=at: (at * blocks + i, 0)), whole((8, LANES))],
                [jax.ShapeDtypeStruct((units, tile), F32), jax.ShapeDtypeStruct((8, LANES), F32)],
                args,
                cost=cost(
                    2 * rows * own * tile * half,
                    4 * half * tile + 4 * rows * own * half,
                    rows * own * half,
                ),
                aliases=aliases,
                limit=36,
            )
        if bit == col_bits[-1]:
            (total,) = add(keep, received, 0)
        else:
            keep, send = add(keep, received, k)

    row_spec, gain_spec = whole((own, block)), whole((1, block))
    sums_spec, back_spec = whole((own, LANES)), whole((k, own, tile))
    sums = call(
        product_kernel,
        (1,),
        [row_spec, gain_spec, back_spec],
        sums_spec,
        jax.ShapeDtypeStruct((own, LANES), F32),
        [stream_mid, mlp_gain, total],
        cost=cost(own * block * 5, own * block * 4),
    )
    for bit in col_bits[:-1]:
        sums = call(
            pair_kernel,
            (1,),
            [sums_spec] * 2,
            sums_spec,
            jax.ShapeDtypeStruct((own, LANES), F32),
            [sums, along(sums, bit)],
            cost=cost(own * LANES, own * LANES * 12),
        )
    gradient = call(
        functools.partial(result_kernel, width),
        (1,),
        [row_spec, row_spec, gain_spec, gain_spec, whole((8, LANES))] + [sums_spec] * 3 + [back_spec],
        row_spec,
        jax.ShapeDtypeStruct((own, block), BF16),
        [block_out, stream_mid, head, mlp_gain, inverse, token, sums, along(sums, col_bits[-1]), total],
        cost=cost(own * block * 14, own * block * 8),
    )
    return (gradient, d_w_down)


def solution(mesh):
    placed = (
        P("row", "col"),
        P("row", "col"),
        P("row", "col"),
        P("row", "col"),
        P("col"),
        P("col"),
        P("col"),
        P("row"),
        P("row"),
        P("row", "col"),
        P("row", "col"),
        P("col", "row"),
    )
    return jax.shard_map(
        local,
        mesh=mesh,
        in_specs=placed,
        out_specs=(P("row", "col"), P("col", "row")),
        check_vma=False,
    )
```

```python
import functools
import math

import jax
import jax.numpy as jnp
from jax import lax
from jax.experimental import pallas as pl
from jax.experimental.pallas import tpu as pltpu
from jax.sharding import PartitionSpec as P

epsilon = 1e-05
LANES = 128
MIB = 1024 * 1024
F32 = jnp.float32
BF16 = jnp.bfloat16


def bits_of(n):
    return [1 << i for i in range(n.bit_length() - 1)]


def block_of(extent, most):
    best = LANES
    for size in range(LANES, most + 1, LANES):
        if extent % size == 0:
            best = size
    return best


ordered = []


def call(kernel, grid, ins, outs, shapes, args, scratch=(), limit=32, cost=None, aliases={}, after=()):
    after = list(after) + ordered[-1:]
    known, extra = len(ins), len(after)

    def body(*refs):
        kernel(*refs[:known], *refs[known + extra :])

    result = pl.pallas_call(
        body,
        grid=grid,
        in_specs=list(ins) + [pl.BlockSpec(memory_space=pl.ANY)] * extra,
        out_specs=outs,
        out_shape=shapes,
        scratch_shapes=list(scratch),
        input_output_aliases=aliases,
        compiler_params=pltpu.CompilerParams(
            dimension_semantics=("arbitrary",) * len(grid), vmem_limit_bytes=limit * MIB
        ),
        cost_estimate=cost,
    )(*args, *after)
    ordered[:] = jax.tree.leaves(result)[-1:]
    return result


def cost(flops, moved, special=0):
    return pl.CostEstimate(flops=int(flops), bytes_accessed=int(moved), transcendentals=int(special))


def whole(shape):
    return pl.BlockSpec(shape, lambda i: (0,) * len(shape))


def column(values, position):
    return values[:, position : position + 1]


def place(columns, rows):
    lane = lax.broadcasted_iota(jnp.int32, (rows, LANES), 1)
    out = jnp.zeros((rows, LANES), F32)
    for position, values in enumerate(columns):
        out = jnp.where(lane == position, values, out)
    return out


def reverse_links(q, links):
    out = q & 1
    for i in range(links):
        out = out | (((q >> (1 + i)) & 1) << (links - i))
    return out


def other_core(j, links):
    return reverse_links(2 * j, links) | 1


def relative(place_ref, k, d):
    return lax.bitwise_xor(lax.bitwise_xor(lax.div(place_ref[0], k), place_ref[1]), d) * k


def label(place_ref, q, links):
    return jnp.where(lax.rem(place_ref[0], 2) == 1, reverse_links(q, links), q)


def slot(place_ref, k, links, d, s):
    own = lax.bitwise_xor(lax.rem(place_ref[0], k), s)
    return label(place_ref, relative(place_ref, k, d) + own, links)


def pack_kernel(out_ref, gain_ref, weight_ref, packed_ref):
    own, block = out_ref.shape
    head = gain_ref[...] * weight_ref[...]
    high = head.astype(BF16)
    rest = head - high.astype(F32)
    middle = rest.astype(BF16)
    low = (rest - middle.astype(F32)).astype(BF16)
    packed_ref[0:own, :] = out_ref[...]
    packed_ref[own:, :] = jnp.concatenate([high, middle, low] + [jnp.zeros((1, block), BF16)] * 13, axis=0)


def turn(values):
    pad = jnp.zeros((LANES - values.shape[0], LANES), F32)
    return jnp.transpose(jnp.concatenate([values, pad], axis=0))


def gradient_rows(rows_of, token, head):
    root, dvalue, product = (column(token, i) for i in range(3))
    return (root * (head * dvalue - rows_of * root * product)).astype(BF16)


def out_kernel(tokens, k, links, place_ref, returns_ref, live_ref, *refs):
    columns = (len(refs) - 2) // (1 + k)
    pieces, outs, (token_ref, held_ref) = refs[:columns], refs[columns:-2], refs[-2:]
    own, block = token_ref.shape[0], pieces[0].shape[1]
    heads = []
    for piece in pieces:
        parts = piece[own : own + 16, :].astype(F32)
        heads.append(parts[0:1] + parts[1:2] + parts[2:3])
    width, tile = block * columns, block // k
    squares = products = jnp.zeros((own, 1), F32)
    for piece, head in zip(pieces, heads):
        wide = piece[0:own, :].astype(F32)
        squares = squares + jnp.sum(wide * wide, axis=1, keepdims=True)
        products = products + jnp.sum(wide * head, axis=1, keepdims=True)
    pad = jnp.zeros((1, LANES - own), F32)
    rows = [returns_ref[...], live_ref[...].astype(F32)]
    rows = [jnp.concatenate([row, pad], axis=1) for row in rows] + [jnp.zeros((6, LANES), F32)]
    rows = turn(jnp.concatenate(rows, axis=0))[0:own]
    factor = tokens * math.sqrt(width)
    count = jnp.sum(column(rows, 1), axis=0, keepdims=True)
    root = lax.rsqrt(squares / width + epsilon)
    value = root * products
    dvalue = column(rows, 1) * (value - column(rows, 0)) * factor
    token = place([root, dvalue, dvalue * value / width], own)
    token_ref[...] = token
    for d in range(columns):
        for s in range(k):
            part = slice(s * tile, (s + 1) * tile)
            held_ref[slot(place_ref, k, links, d, s)] = gradient_rows(
                pieces[d][0:own, part].astype(F32), token, heads[d][:, part]
            )
    for q, out in enumerate(outs):
        out[0:own, :] = held_ref[q]
        out[own:, :] = jnp.broadcast_to(count, (out.shape[0] - own, tile)).astype(BF16)


def gather_kernel(*refs):
    tiles, (out_ref, inverse_ref) = refs[:-2], refs[-2:]
    own = out_ref.shape[1]
    count = 0.0
    for q, ref in enumerate(tiles):
        out_ref[q] = ref[0:own, :]
        count = count + ref[own : own + 16, 0:LANES].astype(F32)
    inverse_ref[...] = 1.0 / count[0:8]


def arrange_kernel(k, links, place_ref, *refs):
    came, (keep_ref, send_ref, held_ref) = refs[:-3], refs[-3:]
    for q, ref in enumerate(came):
        held_ref[q] = ref[...]
    for d in range(len(came) // k):
        for s in range(k):
            (send_ref if d % 2 else keep_ref)[d // 2 * k + s] = held_ref[slot(place_ref, k, links, d, s)]


def partial_kernel(links, d_out_ref, w_ref, keep_ref, send_ref):
    count, own, tile = d_out_ref.shape
    result = lax.dot_general(
        d_out_ref[...].reshape(count * own, tile),
        w_ref[...],
        (((1,), (1,)), ((), ())),
        preferred_element_type=F32,
    ).astype(BF16)
    result = result.reshape(count, own, -1)
    for j in range(count // 2):
        keep_ref[j] = result[2 * j]
        send_ref[j] = result[other_core(j, links)]


def add_kernel(bit, keep_ref, came_ref, *outs):
    sent = kept = 0
    for q in range(keep_ref.shape[0]):
        total = (keep_ref[q].astype(F32) + came_ref[q].astype(F32)).astype(BF16)
        if len(outs) == 2 and q & bit:
            outs[1][sent] = total
            sent += 1
        else:
            outs[0][kept] = total
            kept += 1


def add(keep, came, bit, after=()):
    count, own, extent = keep.shape
    fb = block_of(extent, 2048 if count < 4 else 1024)
    block = pl.BlockSpec((count, own, fb), lambda i: (0, 0, i))
    parts = 2 if bit else 1
    out = pl.BlockSpec((count // parts, own, fb), lambda i: (0, 0, i))
    return call(
        functools.partial(add_kernel, bit),
        (extent // fb,),
        [block, block],
        [out] * parts,
        [jax.ShapeDtypeStruct((count // parts, own, extent), BF16)] * parts,
        [keep, came],
        cost=cost(count * own * extent, 6 * count * own * extent),
        after=after,
    )


def join_kernel(picks, *refs):
    for at, (i, j) in enumerate(picks):
        refs[-1][at] = refs[i][j]


def join(arrays, picks, after=()):
    own, extent = arrays[0].shape[1:]
    fb = block_of(extent, 1024)
    return call(
        functools.partial(join_kernel, picks),
        (extent // fb,),
        [pl.BlockSpec((array.shape[0], own, fb), lambda i: (0, 0, i)) for array in arrays],
        pl.BlockSpec((len(picks), own, fb), lambda i: (0, 0, i)),
        jax.ShapeDtypeStruct((len(picks), own, extent), BF16),
        arrays,
        cost=cost(0, 4 * len(picks) * own * extent),
        after=after,
    )


def every(*arrays):
    return [(i, j) for i, array in enumerate(arrays) for j in range(array.shape[0])]


def stack_kernel(count, *refs):
    for out in refs[count:]:
        for at in range(out.shape[0]):
            out[at] = refs[at][...]


def stack(arrays, own, counts, after=(), limit=32):
    extent = arrays[0].shape[1]
    fb = block_of(extent, 2048)
    return call(
        functools.partial(stack_kernel, len(arrays)),
        (extent // fb,),
        [pl.BlockSpec((own, fb), lambda i: (0, i))] * len(arrays),
        [pl.BlockSpec((count, own, fb), lambda i: (0, 0, i)) for count in counts],
        [jax.ShapeDtypeStruct((count, own, extent), BF16) for count in counts],
        arrays,
        cost=cost(0, 4 * len(arrays) * own * extent),
        after=after,
        limit=limit,
    )


def weight_kernel(links, picks, held, inverse_ref, d_out_ref, *refs):
    out_ref, done_ref = refs[-2:]
    mine, other = refs[:held], refs[held : 2 * held]
    count, own, tile = d_out_ref.shape
    hidden = [None] * count
    for j in range(count // 2):
        for pair, position in ((mine, 2 * j), (other, other_core(j, links))):
            gate, up = (pair[i][at].astype(F32) for i, at in picks[j])
            hidden[position] = (gate * jax.nn.sigmoid(gate) * up).astype(BF16)
    out_ref[...] = inverse_ref[0:1, 0:1] * lax.dot_general(
        jnp.concatenate(hidden, axis=0),
        d_out_ref[...].reshape(count * own, tile),
        (((0,), (0,)), ((), ())),
        preferred_element_type=F32,
    )
    done_ref[...] = jnp.zeros_like(done_ref)


def normed_kernel(links, picks, held, first, last, inverse_ref, w_gate_ref, w_up_ref, *refs):
    total = refs[-1]
    outs = refs[2 * held + (2 if first else 3) : -1]
    mine, other = refs[:held], refs[held : 2 * held]
    mine_grad, other_grad = refs[2 * held : 2 * held + 2]
    before = None if first else refs[2 * held + 2]
    count, own = 2 * mine_grad.shape[0], mine_grad.shape[1]
    step = pl.program_id(0)

    d_gates, d_ups = [None] * count, [None] * count
    for j in range(count // 2):
        for pair, grad, position in (
            (mine, mine_grad, 2 * j),
            (other, other_grad, other_core(j, links)),
        ):
            gate, up = (pair[i][at].astype(F32) for i, at in picks[j])
            sig = jax.nn.sigmoid(gate)
            through = grad[j].astype(F32) * inverse_ref[0:1, 0:1] * sig
            d_gates[position] = (through * up * (1.0 + gate * (1.0 - sig))).astype(BF16)
            d_ups[position] = (through * gate).astype(BF16)
    contracted = (((1,), (1,)), ((), ()))
    result = lax.dot_general(
        jnp.concatenate(d_gates, axis=0), w_gate_ref[...], contracted, preferred_element_type=F32
    ) + lax.dot_general(
        jnp.concatenate(d_ups, axis=0), w_up_ref[...], contracted, preferred_element_type=F32
    )

    @pl.when(step == 0)
    def _():
        total[...] = result if first else before[...] + result

    @pl.when(step > 0)
    def _():
        total[...] += result

    @pl.when(step == pl.num_programs(0) - 1)
    def _():
        if not last:
            outs[0][...] = total[...]
        else:
            for q, out in enumerate(outs):
                out[...] = total[q * own : (q + 1) * own, :].astype(BF16)


def product_kernel(mid_ref, gain_ref, back_ref, sums_ref):
    k, own, tile = back_ref.shape
    products = squares = jnp.zeros((own, 1), F32)
    for s in range(k):
        part = slice(s * tile, (s + 1) * tile)
        middle = mid_ref[:, part].astype(F32)
        products = products + jnp.sum(
            back_ref[s].astype(F32) * gain_ref[:, part] * middle, axis=1, keepdims=True
        )
        squares = squares + jnp.sum(middle * middle, axis=1, keepdims=True)
    sums_ref[...] = place([products, squares], own)


def result_kernel(
    width, block_ref, mid_ref, norm_ref, weight_ref, gain_ref, inverse_ref, token_ref, back_ref, *refs
):
    sums_refs, out_ref = refs[:-1], refs[-1]
    k, own, tile = back_ref.shape
    sums = functools.reduce(lambda a, b: a + b, [ref[...] for ref in sums_refs])
    root = lax.rsqrt(column(sums, 1) / width + epsilon)
    product = column(sums, 0) * root / width
    inverse = inverse_ref[0:1, 0:1]
    token = place([column(token_ref, 0), column(token_ref, 1) * inverse, column(token_ref, 2) * inverse], own)
    for s in range(k):
        part = slice(s * tile, (s + 1) * tile)
        own_d_out = gradient_rows(
            block_ref[:, part].astype(F32), token, norm_ref[:, part] * weight_ref[:, part]
        )
        scaled = back_ref[s].astype(F32) * gain_ref[:, part]
        normalized = mid_ref[:, part].astype(F32) * root
        out_ref[:, part] = (own_d_out.astype(F32) + root * (scaled - normalized * product)).astype(BF16)


def local(
    block_out,
    stream_mid,
    gate_pre,
    up_pre,
    final_gain,
    mlp_gain,
    value_weight,
    returns,
    response_mask,
    w_gate,
    w_up,
    w_down,
):
    rows, cols = lax.axis_size("row"), lax.axis_size("col")
    k = rows // cols
    own, block = block_out.shape
    width = block * cols
    tile = width // rows
    units = gate_pre.shape[1]
    ordered.clear()
    where = jnp.stack([lax.axis_index("row"), lax.axis_index("col")]).astype(jnp.int32)
    smem = pl.BlockSpec(memory_space=pltpu.SMEM)
    final_gain, mlp_gain, value_weight = final_gain[None, :], mlp_gain[None, :], value_weight[None, :]

    link_bits = bits_of(rows)[1:]
    links = len(link_bits)

    def across(values, bit):
        return lax.ppermute(values, "row", [(r, r ^ bit) for r in range(rows)])

    def linked(values, i):
        pairs = [(r, r ^ link_bits[links - 1 - i if r % 2 else i]) for r in range(rows)]
        return lax.ppermute(values, "row", pairs)

    def along(values, bit):
        return lax.ppermute(values, "col", [(c, c ^ bit) for c in range(cols)])

    def exchanged(tiles):
        came = {0: tiles[0]}
        for q in range(1, rows):
            pairs = [(r, r ^ (reverse_links(q, links) if r % 2 else q)) for r in range(rows)]
            came[reverse_links(q, links) if q % 2 else q] = lax.ppermute(tiles[q], "row", pairs)
        return [came[q] for q in range(rows)]

    line = jax.ShapeDtypeStruct((8, LANES), F32)
    packed = call(
        pack_kernel,
        (1,),
        [whole((own, block)), whole((1, block)), whole((1, block))],
        whole((own + 16, block)),
        jax.ShapeDtypeStruct((own + 16, block), BF16),
        [block_out, final_gain, value_weight],
        cost=cost(block, own * block * 4),
        limit=60,
    )
    pieces = [packed] + [along(packed, d) for d in range(1, cols)]

    (paired,) = stack([gate_pre, up_pre], own, [2])
    hop_a = linked(paired, 0)
    hop_b = linked(paired, 1)

    *tiles, token = call(
        functools.partial(out_kernel, own * rows, k, links),
        (1,),
        [smem, whole((1, own)), whole((1, own))]
        + [whole((own + 16, block))] * cols,
        [whole((own + 16, tile))] * rows + [whole((own, LANES))],
        [jax.ShapeDtypeStruct((own + 16, tile), BF16)] * rows + [jax.ShapeDtypeStruct((own, LANES), F32)],
        [where, returns[None, :], response_mask[None, :], *pieces],
        scratch=[pltpu.VMEM((rows, own, tile), BF16)],
        cost=cost(own * width * 10, own * width * 4),
    )
    d_out, inverse = call(
        gather_kernel,
        (1,),
        [whole((own + 16, tile))] * rows,
        [whole((rows, own, tile)), whole((8, LANES))],
        [jax.ShapeDtypeStruct((rows, own, tile), BF16), line],
        exchanged(tiles),
        cost=cost(0, rows * own * tile * 4),
        after=[hop_a, hop_b],
    )

    paired, hop_a, hop_b, d_out = lax.optimization_barrier((paired, hop_a, hop_b, d_out))
    held = [paired, hop_a, hop_b, linked(hop_a, 1)]
    picks = [((i, 0), (i, 1)) for i in range(4)]
    for i in range(2, links):
        picks = picks + [tuple((at + len(held), j) for at, j in pair) for pair in picks]
        held = held + [linked(values, i) for values in held]
    others = [across(values, 1) for values in held]

    lines = units // (2 * LANES)
    sizes = [lines // 3, lines // 3]
    sizes = [size * 2 * LANES for size in sizes + [lines - sum(sizes)]]
    chunks = [(sum(sizes[:i]), size) for i, size in enumerate(sizes)]
    count = rows // 2

    def reduced(number):
        start, extent = chunks[number]
        fb = block_of(math.gcd(start, extent), 1024)
        keep, send = call(
            functools.partial(partial_kernel, links),
            (extent // fb,),
            [
                whole((rows, own, tile)),
                pl.BlockSpec((fb, tile), lambda i, f=start // fb: (f + i, 0)),
            ],
            [pl.BlockSpec((count, own, fb), lambda i: (0, 0, i))] * 2,
            [jax.ShapeDtypeStruct((count, own, extent), BF16)] * 2,
            [d_out, w_down],
            limit=47,
            cost=cost(2 * rows * own * tile * extent, 2 * extent * tile + 2 * rows * own * extent),
            after=waits.get((number, 0), ()),
        )
        received = across(send, 1)
        yield
        for i in range(links):
            keep, send = add(keep, received, 1, waits.get((number, 1 + i), ()))
            received = linked(send, i)
            yield
        (keep,) = add(keep, received, 0, waits.get((number, links + 1), ()))
        for i in range(links):
            came = linked(keep, i)
            yield
            keep = join([keep, came], every(keep, came), waits.get((number, links + 2 + i), ()))
        grads[number] = (keep, across(keep, 1))
        yield

    def normed(number, total):
        start, extent = chunks[number]
        first, last = number == 0, number == len(chunks) - 1
        fb = block_of(math.gcd(start, extent), 1024)
        weights = pl.BlockSpec((tile, fb), lambda i, f=start // fb: (0, f + i))
        ins = (
            [whole((8, LANES)), weights, weights]
            + [
                pl.BlockSpec((values.shape[0], own, fb), lambda i, f=start // fb: (0, 0, f + i))
                for values in held + others
            ]
            + [pl.BlockSpec((count, own, fb), lambda i: (0, 0, i))] * 2
        )
        args = [inverse, w_gate, w_up, *held, *others, *grads[number]]
        if not first:
            ins.append(whole((rows * own, tile)))
            args.append(total)
        shape, kind, parts = ((own, tile), BF16, rows) if last else ((rows * own, tile), F32, 1)
        result = call(
            functools.partial(normed_kernel, links, picks, len(held), first, last),
            (extent // fb,),
            ins,
            [whole(shape)] * parts,
            [jax.ShapeDtypeStruct(shape, kind)] * parts,
            args,
            scratch=[pltpu.VMEM((rows * own, tile), F32)],
            limit=36,
            cost=cost(
                4 * rows * own * tile * extent,
                4 * extent * tile + 6 * rows * own * extent,
                rows * own * extent,
            ),
        )
        return result if last else result[0]

    waits = {
        (1, 0): others[:1],
        (2, 0): others[1:3],
        (0, links): held[3:4],
        (0, links + 1): others[3:4],
    }
    grads, total = {}, None
    chains = [reduced(number) for number in range(len(chunks))]
    for _ in range(2 * links + 1):
        for chain in chains:
            next(chain)
    next(chains[0])
    total = normed(0, total)
    for chain in chains[1:]:
        next(chain)
    for number in range(1, len(chunks)):
        total = normed(number, total)

    keep, send = call(
        functools.partial(arrange_kernel, k, links),
        (1,),
        [smem] + [whole((own, tile))] * rows,
        [whole((count, own, tile))] * 2,
        [jax.ShapeDtypeStruct((count, own, tile), BF16)] * 2,
        [where, *exchanged(total)],
        scratch=[pltpu.VMEM((rows, own, tile), BF16)],
        cost=cost(0, rows * own * tile * 4),
    )
    half = units // 2
    fb = block_of(half, 1024)
    blocks = half // fb
    d_w_down = None
    col_bits = bits_of(cols)
    for at, bit in enumerate(col_bits):
        received = along(send, bit)
        if at < 2:
            ins = [whole((8, LANES)), whole((rows, own, tile))] + [
                pl.BlockSpec((values.shape[0], own, fb), lambda i, at=at: (0, 0, at * blocks + i))
                for values in held + others
            ]
            args = [inverse, d_out, *held, *others]
            aliases = {}
            if at:
                ins.append(pl.BlockSpec(memory_space=pl.ANY))
                args.append(d_w_down)
                aliases = {len(args) - 1: 0}
            d_w_down, _ = call(
                functools.partial(weight_kernel, links, picks, len(held)),
                (blocks,),
                ins,
                [pl.BlockSpec((fb, tile), lambda i, at=at: (at * blocks + i, 0)), whole((8, LANES))],
                [jax.ShapeDtypeStruct((units, tile), F32), jax.ShapeDtypeStruct((8, LANES), F32)],
                args,
                cost=cost(
                    2 * rows * own * tile * half,
                    4 * half * tile + 4 * rows * own * half,
                    rows * own * half,
                ),
                aliases=aliases,
                limit=36,
            )
        if bit == col_bits[-1]:
            (total,) = add(keep, received, 0)
        else:
            keep, send = add(keep, received, k)

    row_spec, gain_spec = whole((own, block)), whole((1, block))
    sums_spec, back_spec = whole((own, LANES)), whole((k, own, tile))
    sums = call(
        product_kernel,
        (1,),
        [row_spec, gain_spec, back_spec],
        sums_spec,
        jax.ShapeDtypeStruct((own, LANES), F32),
        [stream_mid, mlp_gain, total],
        cost=cost(own * block * 5, own * block * 4),
    )
    gradient = call(
        functools.partial(result_kernel, width),
        (1,),
        [row_spec, row_spec] + [gain_spec] * 3 + [whole((8, LANES)), sums_spec, back_spec] + [sums_spec] * cols,
        row_spec,
        jax.ShapeDtypeStruct((own, block), BF16),
        [block_out, stream_mid, final_gain, value_weight, mlp_gain, inverse, token, total, sums]
        + [along(sums, d) for d in range(1, cols)],
        cost=cost(own * block * 14, own * block * 8),
    )
    return (gradient, d_w_down)


def solution(mesh):
    placed = (
        P("row", "col"),
        P("row", "col"),
        P("row", "col"),
        P("row", "col"),
        P("col"),
        P("col"),
        P("col"),
        P("row"),
        P("row"),
        P("row", "col"),
        P("row", "col"),
        P("col", "row"),
    )
    return jax.shard_map(
        local,
        mesh=mesh,
        in_specs=placed,
        out_specs=(P("row", "col"), P("col", "row")),
        check_vma=False,
    )
```

```python
import functools
import math

import jax
import jax.numpy as jnp
from jax import lax
from jax.experimental import pallas as pl
from jax.experimental.pallas import tpu as pltpu
from jax.sharding import PartitionSpec as P

epsilon = 1e-05
LANES = 128
MIB = 1024 * 1024
F32 = jnp.float32
BF16 = jnp.bfloat16


def bits_of(n):
    return [1 << i for i in range(n.bit_length() - 1)]


def block_of(extent, most):
    best = LANES
    for size in range(LANES, most + 1, LANES):
        if extent % size == 0:
            best = size
    return best


ordered = []


def call(kernel, grid, ins, outs, shapes, args, scratch=(), limit=32, cost=None, aliases={}, after=()):
    after = list(after) + ordered[-1:]
    known, extra = len(ins), len(after)

    def body(*refs):
        kernel(*refs[:known], *refs[known + extra :])

    result = pl.pallas_call(
        body,
        grid=grid,
        in_specs=list(ins) + [pl.BlockSpec(memory_space=pl.ANY)] * extra,
        out_specs=outs,
        out_shape=shapes,
        scratch_shapes=list(scratch),
        input_output_aliases=aliases,
        compiler_params=pltpu.CompilerParams(
            dimension_semantics=("arbitrary",) * len(grid), vmem_limit_bytes=limit * MIB
        ),
        cost_estimate=cost,
    )(*args, *after)
    ordered[:] = jax.tree.leaves(result)[-1:]
    return result


def cost(flops, moved, special=0):
    return pl.CostEstimate(flops=int(flops), bytes_accessed=int(moved), transcendentals=int(special))


def whole(shape):
    return pl.BlockSpec(shape, lambda i: (0,) * len(shape))


def column(values, position):
    return values[:, position : position + 1]


def place(columns, rows):
    lane = lax.broadcasted_iota(jnp.int32, (rows, LANES), 1)
    out = jnp.zeros((rows, LANES), F32)
    for position, values in enumerate(columns):
        out = jnp.where(lane == position, values, out)
    return out


def reverse_links(q, links):
    out = q & 1
    for i in range(links):
        out = out | (((q >> (1 + i)) & 1) << (links - i))
    return out


def other_core(j, links):
    return reverse_links(2 * j, links) | 1


def relative(place_ref, k, d):
    return lax.bitwise_xor(lax.bitwise_xor(lax.div(place_ref[0], k), place_ref[1]), d) * k


def label(place_ref, q, links):
    return jnp.where(lax.rem(place_ref[0], 2) == 1, reverse_links(q, links), q)


def slot(place_ref, k, links, d, s):
    own = lax.bitwise_xor(lax.rem(place_ref[0], k), s)
    return label(place_ref, relative(place_ref, k, d) + own, links)


def pack_kernel(out_ref, gain_ref, weight_ref, packed_ref):
    own, block = out_ref.shape
    head = gain_ref[...] * weight_ref[...]
    high = head.astype(BF16)
    rest = head - high.astype(F32)
    middle = rest.astype(BF16)
    low = (rest - middle.astype(F32)).astype(BF16)
    packed_ref[0:own, :] = out_ref[...]
    packed_ref[own:, :] = jnp.concatenate([high, middle, low] + [jnp.zeros((1, block), BF16)] * 13, axis=0)


def turn(values):
    pad = jnp.zeros((LANES - values.shape[0], LANES), F32)
    return jnp.transpose(jnp.concatenate([values, pad], axis=0))


def gradient_rows(rows_of, token, head):
    root, dvalue, product = (column(token, i) for i in range(3))
    return (root * (head * dvalue - rows_of * root * product)).astype(BF16)


def out_kernel(tokens, k, links, place_ref, returns_ref, live_ref, *refs):
    columns = (len(refs) - 2) // (1 + k)
    pieces, outs, (token_ref, held_ref) = refs[:columns], refs[columns:-2], refs[-2:]
    own, block = token_ref.shape[0], pieces[0].shape[1]
    heads = []
    for piece in pieces:
        parts = piece[own : own + 16, :].astype(F32)
        heads.append(parts[0:1] + parts[1:2] + parts[2:3])
    width, tile = block * columns, block // k
    squares = products = jnp.zeros((own, 1), F32)
    for piece, head in zip(pieces, heads):
        wide = piece[0:own, :].astype(F32)
        squares = squares + jnp.sum(wide * wide, axis=1, keepdims=True)
        products = products + jnp.sum(wide * head, axis=1, keepdims=True)
    pad = jnp.zeros((1, LANES - own), F32)
    rows = [returns_ref[...], live_ref[...].astype(F32)]
    rows = [jnp.concatenate([row, pad], axis=1) for row in rows] + [jnp.zeros((6, LANES), F32)]
    rows = turn(jnp.concatenate(rows, axis=0))[0:own]
    factor = tokens * math.sqrt(width)
    root = lax.rsqrt(squares / width + epsilon)
    value = root * products
    dvalue = column(rows, 1) * (value - column(rows, 0)) * factor
    token = place([root, dvalue, dvalue * value / width], own)
    token_ref[...] = token
    for d in range(columns):
        for s in range(k):
            part = slice(s * tile, (s + 1) * tile)
            held_ref[slot(place_ref, k, links, d, s)] = gradient_rows(
                pieces[d][0:own, part].astype(F32), token, heads[d][:, part]
            )
    for q, out in enumerate(outs):
        out[...] = held_ref[q]


def pair_kernel(gate_ref, up_ref, live_ref, out_ref):
    own, units = gate_ref.shape
    out_ref[0, :, 0:units] = gate_ref[...]
    out_ref[1, :, 0:units] = up_ref[...]
    live = jnp.concatenate([live_ref[...].astype(F32), jnp.zeros((1, LANES - own), F32)], axis=1)
    live = turn(jnp.concatenate([live, jnp.zeros((7, LANES), F32)], axis=0))[0:own].astype(BF16)
    out_ref[0, :, units:] = live
    out_ref[1, :, units:] = live


def inverse_kernel(*refs):
    total = functools.reduce(lambda a, b: a + b, [ref[0].astype(F32) for ref in refs[:-1]])
    count = jnp.sum(column(total, 0), axis=0, keepdims=True)
    refs[-1][...] = jnp.broadcast_to(1.0 / count, refs[-1].shape)


def arrange_kernel(k, links, place_ref, *refs):
    came, (keep_ref, send_ref, held_ref) = refs[:-3], refs[-3:]
    for q, ref in enumerate(came):
        held_ref[q] = ref[...]
    for d in range(len(came) // k):
        for s in range(k):
            (send_ref if d % 2 else keep_ref)[d // 2 * k + s] = held_ref[slot(place_ref, k, links, d, s)]


def partial_kernel(links, d_out_ref, w_ref, keep_ref, send_ref):
    count, own, tile = d_out_ref.shape
    result = lax.dot_general(
        d_out_ref[...].reshape(count * own, tile),
        w_ref[...],
        (((1,), (1,)), ((), ())),
        preferred_element_type=F32,
    ).astype(BF16)
    result = result.reshape(count, own, -1)
    for j in range(count // 2):
        keep_ref[j] = result[2 * j]
        send_ref[j] = result[other_core(j, links)]


def add_kernel(bit, keep_ref, came_ref, *outs):
    sent = kept = 0
    for q in range(keep_ref.shape[0]):
        total = (keep_ref[q].astype(F32) + came_ref[q].astype(F32)).astype(BF16)
        if len(outs) == 2 and q & bit:
            outs[1][sent] = total
            sent += 1
        else:
            outs[0][kept] = total
            kept += 1


def add(keep, came, bit, after=()):
    count, own, extent = keep.shape
    fb = block_of(extent, 2048 if count < 4 else 1024)
    block = pl.BlockSpec((count, own, fb), lambda i: (0, 0, i))
    parts = 2 if bit else 1
    out = pl.BlockSpec((count // parts, own, fb), lambda i: (0, 0, i))
    return call(
        functools.partial(add_kernel, bit),
        (extent // fb,),
        [block, block],
        [out] * parts,
        [jax.ShapeDtypeStruct((count // parts, own, extent), BF16)] * parts,
        [keep, came],
        cost=cost(count * own * extent, 6 * count * own * extent),
        after=after,
    )


def join_kernel(picks, *refs):
    for at, (i, j) in enumerate(picks):
        refs[-1][at] = refs[i][j]


def join(arrays, picks, after=()):
    own, extent = arrays[0].shape[1:]
    fb = block_of(extent, 1024)
    return call(
        functools.partial(join_kernel, picks),
        (extent // fb,),
        [pl.BlockSpec((array.shape[0], own, fb), lambda i: (0, 0, i)) for array in arrays],
        pl.BlockSpec((len(picks), own, fb), lambda i: (0, 0, i)),
        jax.ShapeDtypeStruct((len(picks), own, extent), BF16),
        arrays,
        cost=cost(0, 4 * len(picks) * own * extent),
        after=after,
    )


def every(*arrays):
    return [(i, j) for i, array in enumerate(arrays) for j in range(array.shape[0])]


def stack_kernel(count, *refs):
    for out in refs[count:]:
        for at in range(out.shape[0]):
            out[at] = refs[at][...]


def stack(arrays, own, counts, after=(), limit=32):
    extent = arrays[0].shape[1]
    fb = block_of(extent, 2048)
    return call(
        functools.partial(stack_kernel, len(arrays)),
        (extent // fb,),
        [pl.BlockSpec((own, fb), lambda i: (0, i))] * len(arrays),
        [pl.BlockSpec((count, own, fb), lambda i: (0, 0, i)) for count in counts],
        [jax.ShapeDtypeStruct((count, own, extent), BF16) for count in counts],
        arrays,
        cost=cost(0, 4 * len(arrays) * own * extent),
        after=after,
        limit=limit,
    )


def weight_kernel(links, picks, held, inverse_ref, d_out_ref, *refs):
    out_ref, done_ref = refs[-2:]
    mine, other = refs[:held], refs[held : 2 * held]
    count, own, tile = d_out_ref.shape
    hidden = [None] * count
    for j in range(count // 2):
        for pair, position in ((mine, 2 * j), (other, other_core(j, links))):
            gate, up = (pair[i][at].astype(F32) for i, at in picks[j])
            hidden[position] = (gate * jax.nn.sigmoid(gate) * up).astype(BF16)
    out_ref[...] = inverse_ref[0:1, 0:1] * lax.dot_general(
        jnp.concatenate(hidden, axis=0),
        d_out_ref[...].reshape(count * own, tile),
        (((0,), (0,)), ((), ())),
        preferred_element_type=F32,
    )
    done_ref[...] = jnp.zeros_like(done_ref)


def normed_kernel(links, picks, held, first, last, inverse_ref, w_gate_ref, w_up_ref, *refs):
    total = refs[-1]
    outs = refs[2 * held + (2 if first else 3) : -1]
    mine, other = refs[:held], refs[held : 2 * held]
    mine_grad, other_grad = refs[2 * held : 2 * held + 2]
    before = None if first else refs[2 * held + 2]
    count, own = 2 * mine_grad.shape[0], mine_grad.shape[1]
    step = pl.program_id(0)

    d_gates, d_ups = [None] * count, [None] * count
    for j in range(count // 2):
        for pair, grad, position in (
            (mine, mine_grad, 2 * j),
            (other, other_grad, other_core(j, links)),
        ):
            gate, up = (pair[i][at].astype(F32) for i, at in picks[j])
            sig = jax.nn.sigmoid(gate)
            through = grad[j].astype(F32) * inverse_ref[0:1, 0:1] * sig
            d_gates[position] = (through * up * (1.0 + gate * (1.0 - sig))).astype(BF16)
            d_ups[position] = (through * gate).astype(BF16)
    contracted = (((1,), (1,)), ((), ()))
    result = lax.dot_general(
        jnp.concatenate(d_gates, axis=0), w_gate_ref[...], contracted, preferred_element_type=F32
    ) + lax.dot_general(
        jnp.concatenate(d_ups, axis=0), w_up_ref[...], contracted, preferred_element_type=F32
    )

    @pl.when(step == 0)
    def _():
        total[...] = result if first else before[...] + result

    @pl.when(step > 0)
    def _():
        total[...] += result

    @pl.when(step == pl.num_programs(0) - 1)
    def _():
        if not last:
            outs[0][...] = total[...]
        else:
            for q, out in enumerate(outs):
                out[...] = total[q * own : (q + 1) * own, :].astype(BF16)


def product_kernel(mid_ref, gain_ref, back_ref, sums_ref):
    k, own, tile = back_ref.shape
    products = squares = jnp.zeros((own, 1), F32)
    for s in range(k):
        part = slice(s * tile, (s + 1) * tile)
        middle = mid_ref[:, part].astype(F32)
        products = products + jnp.sum(
            back_ref[s].astype(F32) * gain_ref[:, part] * middle, axis=1, keepdims=True
        )
        squares = squares + jnp.sum(middle * middle, axis=1, keepdims=True)
    sums_ref[...] = place([products, squares], own)


def result_kernel(
    width, block_ref, mid_ref, norm_ref, weight_ref, gain_ref, inverse_ref, token_ref, back_ref, *refs
):
    sums_refs, out_ref = refs[:-1], refs[-1]
    k, own, tile = back_ref.shape
    sums = functools.reduce(lambda a, b: a + b, [ref[...] for ref in sums_refs])
    root = lax.rsqrt(column(sums, 1) / width + epsilon)
    product = column(sums, 0) * root / width
    inverse = inverse_ref[0:1, 0:1]
    token = place([column(token_ref, 0), column(token_ref, 1) * inverse, column(token_ref, 2) * inverse], own)
    for s in range(k):
        part = slice(s * tile, (s + 1) * tile)
        own_d_out = gradient_rows(
            block_ref[:, part].astype(F32), token, norm_ref[:, part] * weight_ref[:, part]
        )
        scaled = back_ref[s].astype(F32) * gain_ref[:, part]
        normalized = mid_ref[:, part].astype(F32) * root
        out_ref[:, part] = (own_d_out.astype(F32) + root * (scaled - normalized * product)).astype(BF16)


def local(
    block_out,
    stream_mid,
    gate_pre,
    up_pre,
    final_gain,
    mlp_gain,
    value_weight,
    returns,
    response_mask,
    w_gate,
    w_up,
    w_down,
):
    rows, cols = lax.axis_size("row"), lax.axis_size("col")
    k = rows // cols
    own, block = block_out.shape
    width = block * cols
    tile = width // rows
    units = gate_pre.shape[1]
    ordered.clear()
    where = jnp.stack([lax.axis_index("row"), lax.axis_index("col")]).astype(jnp.int32)
    smem = pl.BlockSpec(memory_space=pltpu.SMEM)
    final_gain, mlp_gain, value_weight = final_gain[None, :], mlp_gain[None, :], value_weight[None, :]

    link_bits = bits_of(rows)[1:]
    links = len(link_bits)

    def across(values, bit):
        return lax.ppermute(values, "row", [(r, r ^ bit) for r in range(rows)])

    def linked(values, i):
        pairs = [(r, r ^ link_bits[links - 1 - i if r % 2 else i]) for r in range(rows)]
        return lax.ppermute(values, "row", pairs)

    def along(values, bit):
        return lax.ppermute(values, "col", [(c, c ^ bit) for c in range(cols)])

    def exchanged(tiles):
        came = {0: tiles[0]}
        for q in range(1, rows):
            pairs = [(r, r ^ (reverse_links(q, links) if r % 2 else q)) for r in range(rows)]
            came[reverse_links(q, links) if q % 2 else q] = lax.ppermute(tiles[q], "row", pairs)
        return [came[q] for q in range(rows)]

    packed = call(
        pack_kernel,
        (1,),
        [whole((own, block)), whole((1, block)), whole((1, block))],
        whole((own + 16, block)),
        jax.ShapeDtypeStruct((own + 16, block), BF16),
        [block_out, final_gain, value_weight],
        cost=cost(block, own * block * 4),
        limit=60,
    )
    pieces = [packed] + [along(packed, d) for d in range(1, cols)]

    paired = call(
        pair_kernel,
        (1,),
        [whole((own, units)), whole((own, units)), whole((1, own))],
        whole((2, own, units + LANES)),
        jax.ShapeDtypeStruct((2, own, units + LANES), BF16),
        [gate_pre, up_pre, response_mask[None, :]],
        cost=cost(0, own * units * 8),
    )
    hop_a = linked(paired, 0)
    hop_b = linked(paired, 1)

    *tiles, token = call(
        functools.partial(out_kernel, own * rows, k, links),
        (1,),
        [smem, whole((1, own)), whole((1, own))]
        + [whole((own + 16, block))] * cols,
        [whole((own, tile))] * rows + [whole((own, LANES))],
        [jax.ShapeDtypeStruct((own, tile), BF16)] * rows + [jax.ShapeDtypeStruct((own, LANES), F32)],
        [where, returns[None, :], response_mask[None, :], *pieces],
        scratch=[pltpu.VMEM((rows, own, tile), BF16)],
        cost=cost(own * width * 10, own * width * 4),
    )
    (d_out,) = stack(exchanged(tiles), own, [rows], after=[hop_a, hop_b])

    paired, hop_a, hop_b, d_out = lax.optimization_barrier((paired, hop_a, hop_b, d_out))
    held = [paired, hop_a, hop_b, linked(hop_a, 1)]
    picks = [((i, 0), (i, 1)) for i in range(4)]
    for i in range(2, links):
        picks = picks + [tuple((at + len(held), j) for at, j in pair) for pair in picks]
        held = held + [linked(values, i) for values in held]
    others = [across(values, 1) for values in held[:3]]

    lines = units // (2 * LANES)
    sizes = [lines * 3 // 7, lines * 2 // 7]
    sizes = [size * 2 * LANES for size in sizes + [lines - sum(sizes)]]
    chunks = [(sum(sizes[:i]), size) for i, size in enumerate(sizes)]
    count = rows // 2

    def reduced(number):
        start, extent = chunks[number]
        fb = block_of(math.gcd(start, extent), 1024)
        keep, send = call(
            functools.partial(partial_kernel, links),
            (extent // fb,),
            [
                whole((rows, own, tile)),
                pl.BlockSpec((fb, tile), lambda i, f=start // fb: (f + i, 0)),
            ],
            [pl.BlockSpec((count, own, fb), lambda i: (0, 0, i))] * 2,
            [jax.ShapeDtypeStruct((count, own, extent), BF16)] * 2,
            [d_out, w_down],
            limit=44,
            cost=cost(2 * rows * own * tile * extent, 2 * extent * tile + 2 * rows * own * extent),
            after=waits.get((number, 0), ()),
        )
        received = across(send, 1)
        yield
        for i in range(links):
            keep, send = add(keep, received, 1, waits.get((number, 1 + i), ()))
            received = linked(send, i)
            yield
        (keep,) = add(keep, received, 0, waits.get((number, links + 1), ()))
        for i in range(links):
            came = linked(keep, i)
            yield
            keep = join([keep, came], every(keep, came), waits.get((number, links + 2 + i), ()))
        grads[number] = (keep, across(keep, 1))
        yield

    def normed(number, total):
        start, extent = chunks[number]
        first, last = number == 0, number == len(chunks) - 1
        fb = block_of(math.gcd(start, extent), 1024)
        weights = pl.BlockSpec((tile, fb), lambda i, f=start // fb: (0, f + i))
        ins = (
            [whole((8, LANES)), weights, weights]
            + [
                pl.BlockSpec((values.shape[0], own, fb), lambda i, f=start // fb: (0, 0, f + i))
                for values in held + others
            ]
            + [pl.BlockSpec((count, own, fb), lambda i: (0, 0, i))] * 2
        )
        args = [inverse, w_gate, w_up, *held, *others, *grads[number]]
        if not first:
            ins.append(whole((rows * own, tile)))
            args.append(total)
        shape, kind, parts = ((own, tile), BF16, rows) if last else ((rows * own, tile), F32, 1)
        result = call(
            functools.partial(normed_kernel, links, picks, len(held), first, last),
            (extent // fb,),
            ins,
            [whole(shape)] * parts,
            [jax.ShapeDtypeStruct(shape, kind)] * parts,
            args,
            scratch=[pltpu.VMEM((rows * own, tile), F32)],
            limit=36,
            cost=cost(
                4 * rows * own * tile * extent,
                4 * extent * tile + 6 * rows * own * extent,
                rows * own * extent,
            ),
        )
        return result if last else result[0]

    waits = {
        (1, 0): others[:1],
        (2, 0): others[1:3],
        (0, links): held[3:4],
    }
    grads, total = {}, None
    chains = [reduced(number) for number in range(len(chunks))]
    for step in range(2 * links + 1):
        for chain in chains:
            next(chain)
        if step == 0:
            late, _ = lax.optimization_barrier((held[3:], ordered[0]))
            others = others + [across(values, 1) for values in late]
            waits[0, links + 1] = others[3:4]
        if step == links + 1:
            inverse = call(
                inverse_kernel,
                (1,),
                [pl.BlockSpec((2, own, LANES), lambda i: (0, 0, units // LANES))] * (2 * len(held)),
                whole((8, LANES)),
                jax.ShapeDtypeStruct((8, LANES), F32),
                [*held, *others],
                cost=cost(0, rows * own * LANES * 4),
            )
    next(chains[0])
    total = normed(0, total)
    for chain in chains[1:]:
        next(chain)
    for number in range(1, len(chunks)):
        total = normed(number, total)

    keep, send = call(
        functools.partial(arrange_kernel, k, links),
        (1,),
        [smem] + [whole((own, tile))] * rows,
        [whole((count, own, tile))] * 2,
        [jax.ShapeDtypeStruct((count, own, tile), BF16)] * 2,
        [where, *exchanged(total)],
        scratch=[pltpu.VMEM((rows, own, tile), BF16)],
        cost=cost(0, rows * own * tile * 4),
    )
    half = units // 2
    fb = block_of(half, 1024)
    blocks = half // fb
    d_w_down = None
    col_bits = bits_of(cols)
    for at, bit in enumerate(col_bits):
        received = along(send, bit)
        if at < 2:
            ins = [whole((8, LANES)), whole((rows, own, tile))] + [
                pl.BlockSpec((values.shape[0], own, fb), lambda i, at=at: (0, 0, at * blocks + i))
                for values in held + others
            ]
            args = [inverse, d_out, *held, *others]
            aliases = {}
            if at:
                ins.append(pl.BlockSpec(memory_space=pl.ANY))
                args.append(d_w_down)
                aliases = {len(args) - 1: 0}
            d_w_down, _ = call(
                functools.partial(weight_kernel, links, picks, len(held)),
                (blocks,),
                ins,
                [pl.BlockSpec((fb, tile), lambda i, at=at: (at * blocks + i, 0)), whole((8, LANES))],
                [jax.ShapeDtypeStruct((units, tile), F32), jax.ShapeDtypeStruct((8, LANES), F32)],
                args,
                cost=cost(
                    2 * rows * own * tile * half,
                    4 * half * tile + 4 * rows * own * half,
                    rows * own * half,
                ),
                aliases=aliases,
                limit=36,
            )
        if bit == col_bits[-1]:
            (total,) = add(keep, received, 0)
        else:
            keep, send = add(keep, received, k)

    row_spec, gain_spec = whole((own, block)), whole((1, block))
    sums_spec, back_spec = whole((own, LANES)), whole((k, own, tile))
    sums = call(
        product_kernel,
        (1,),
        [row_spec, gain_spec, back_spec],
        sums_spec,
        jax.ShapeDtypeStruct((own, LANES), F32),
        [stream_mid, mlp_gain, total],
        cost=cost(own * block * 5, own * block * 4),
    )
    gradient = call(
        functools.partial(result_kernel, width),
        (1,),
        [row_spec, row_spec] + [gain_spec] * 3 + [whole((8, LANES)), sums_spec, back_spec] + [sums_spec] * cols,
        row_spec,
        jax.ShapeDtypeStruct((own, block), BF16),
        [block_out, stream_mid, final_gain, value_weight, mlp_gain, inverse, token, total, sums]
        + [along(sums, d) for d in range(1, cols)],
        cost=cost(own * block * 14, own * block * 8),
    )
    return (gradient, d_w_down)


def solution(mesh):
    placed = (
        P("row", "col"),
        P("row", "col"),
        P("row", "col"),
        P("row", "col"),
        P("col"),
        P("col"),
        P("col"),
        P("row"),
        P("row"),
        P("row", "col"),
        P("row", "col"),
        P("col", "row"),
    )
    return jax.shard_map(
        local,
        mesh=mesh,
        in_specs=placed,
        out_specs=(P("row", "col"), P("col", "row")),
        check_vma=False,
    )
```

```python
import functools
import math

import jax
import jax.numpy as jnp
from jax import lax
from jax.experimental import pallas as pl
from jax.experimental.pallas import tpu as pltpu
from jax.sharding import PartitionSpec as P

epsilon = 1e-05
LANES = 128
MIB = 1024 * 1024
F32 = jnp.float32
BF16 = jnp.bfloat16


def bits_of(n):
    return [1 << i for i in range(n.bit_length() - 1)]


def block_of(extent, most):
    best = LANES
    for size in range(LANES, most + 1, LANES):
        if extent % size == 0:
            best = size
    return best


ordered = []


def call(kernel, grid, ins, outs, shapes, args, scratch=(), limit=32, cost=None, aliases={}, after=()):
    after = list(after) + ordered[-1:]
    known, extra = len(ins), len(after)

    def body(*refs):
        kernel(*refs[:known], *refs[known + extra :])

    result = pl.pallas_call(
        body,
        grid=grid,
        in_specs=list(ins) + [pl.BlockSpec(memory_space=pl.ANY)] * extra,
        out_specs=outs,
        out_shape=shapes,
        scratch_shapes=list(scratch),
        input_output_aliases=aliases,
        compiler_params=pltpu.CompilerParams(
            dimension_semantics=("arbitrary",) * len(grid), vmem_limit_bytes=limit * MIB
        ),
        cost_estimate=cost,
    )(*args, *after)
    ordered[:] = jax.tree.leaves(result)[-1:]
    return result


def cost(flops, moved, special=0):
    return pl.CostEstimate(flops=int(flops), bytes_accessed=int(moved), transcendentals=int(special))


def whole(shape):
    return pl.BlockSpec(shape, lambda i: (0,) * len(shape))


def column(values, position):
    return values[:, position : position + 1]


def place(columns, rows):
    lane = lax.broadcasted_iota(jnp.int32, (rows, LANES), 1)
    out = jnp.zeros((rows, LANES), F32)
    for position, values in enumerate(columns):
        out = jnp.where(lane == position, values, out)
    return out


def reverse_links(q, links):
    out = q & 1
    for i in range(links):
        out = out | (((q >> (1 + i)) & 1) << (links - i))
    return out


def other_core(j, links):
    return reverse_links(2 * j, links) | 1


def relative(place_ref, k, d):
    return lax.bitwise_xor(lax.bitwise_xor(lax.div(place_ref[0], k), place_ref[1]), d) * k


def label(place_ref, q, links):
    return jnp.where(lax.rem(place_ref[0], 2) == 1, reverse_links(q, links), q)


def slot(place_ref, k, links, d, s):
    own = lax.bitwise_xor(lax.rem(place_ref[0], k), s)
    return label(place_ref, relative(place_ref, k, d) + own, links)


def pack_kernel(out_ref, gain_ref, weight_ref, packed_ref):
    own, block = out_ref.shape
    head = gain_ref[...] * weight_ref[...]
    high = head.astype(BF16)
    rest = head - high.astype(F32)
    middle = rest.astype(BF16)
    low = (rest - middle.astype(F32)).astype(BF16)
    packed_ref[0:own, :] = out_ref[...]
    packed_ref[own:, :] = jnp.concatenate([high, middle, low] + [jnp.zeros((1, block), BF16)] * 13, axis=0)


def turn(values):
    pad = jnp.zeros((LANES - values.shape[0], LANES), F32)
    return jnp.transpose(jnp.concatenate([values, pad], axis=0))


def gradient_rows(rows_of, token, head):
    root, dvalue, product = (column(token, i) for i in range(3))
    return (root * (head * dvalue - rows_of * root * product)).astype(BF16)


def out_kernel(tokens, k, links, place_ref, returns_ref, live_ref, *refs):
    columns = (len(refs) - 2) // (1 + k)
    pieces, outs, (token_ref, held_ref) = refs[:columns], refs[columns:-2], refs[-2:]
    own, block = token_ref.shape[0], pieces[0].shape[1]
    heads = []
    for piece in pieces:
        parts = piece[own : own + 16, :].astype(F32)
        heads.append(parts[0:1] + parts[1:2] + parts[2:3])
    width, tile = block * columns, block // k
    squares = products = jnp.zeros((own, 1), F32)
    for piece, head in zip(pieces, heads):
        wide = piece[0:own, :].astype(F32)
        squares = squares + jnp.sum(wide * wide, axis=1, keepdims=True)
        products = products + jnp.sum(wide * head, axis=1, keepdims=True)
    pad = jnp.zeros((1, LANES - own), F32)
    rows = [returns_ref[...], live_ref[...].astype(F32)]
    rows = [jnp.concatenate([row, pad], axis=1) for row in rows] + [jnp.zeros((6, LANES), F32)]
    rows = turn(jnp.concatenate(rows, axis=0))[0:own]
    factor = tokens * math.sqrt(width)
    root = lax.rsqrt(squares / width + epsilon)
    value = root * products
    dvalue = column(rows, 1) * (value - column(rows, 0)) * factor
    token = place([root, dvalue, dvalue * value / width], own)
    token_ref[...] = token
    for d in range(columns):
        for s in range(k):
            part = slice(s * tile, (s + 1) * tile)
            held_ref[slot(place_ref, k, links, d, s)] = gradient_rows(
                pieces[d][0:own, part].astype(F32), token, heads[d][:, part]
            )
    for q, out in enumerate(outs):
        out[...] = held_ref[q]


def pair_kernel(gate_ref, up_ref, live_ref, out_ref):
    own, units = gate_ref.shape
    out_ref[0, :, 0:units] = gate_ref[...]
    out_ref[1, :, 0:units] = up_ref[...]
    live = jnp.concatenate([live_ref[...].astype(F32), jnp.zeros((1, LANES - own), F32)], axis=1)
    live = turn(jnp.concatenate([live, jnp.zeros((7, LANES), F32)], axis=0))[0:own].astype(BF16)
    out_ref[0, :, units:] = live
    out_ref[1, :, units:] = live


def inverse_kernel(*refs):
    total = functools.reduce(lambda a, b: a + b, [ref[0].astype(F32) for ref in refs[:-1]])
    count = jnp.sum(column(total, 0), axis=0, keepdims=True)
    refs[-1][...] = jnp.broadcast_to(1.0 / count, refs[-1].shape)


def arrange_kernel(k, links, place_ref, *refs):
    came, (keep_ref, send_ref, held_ref) = refs[:-3], refs[-3:]
    for q, ref in enumerate(came):
        held_ref[q] = ref[...]
    for d in range(len(came) // k):
        for s in range(k):
            (send_ref if d % 2 else keep_ref)[d // 2 * k + s] = held_ref[slot(place_ref, k, links, d, s)]


def partial_kernel(links, d_out_ref, w_ref, keep_ref, send_ref):
    count, own, tile = d_out_ref.shape
    result = lax.dot_general(
        d_out_ref[...].reshape(count * own, tile),
        w_ref[...],
        (((1,), (1,)), ((), ())),
        preferred_element_type=F32,
    ).astype(BF16)
    result = result.reshape(count, own, -1)
    for j in range(count // 2):
        keep_ref[j] = result[2 * j]
        send_ref[j] = result[other_core(j, links)]


def add_kernel(bit, keep_ref, came_ref, *outs):
    sent = kept = 0
    for q in range(keep_ref.shape[0]):
        total = (keep_ref[q].astype(F32) + came_ref[q].astype(F32)).astype(BF16)
        if len(outs) == 2 and q & bit:
            outs[1][sent] = total
            sent += 1
        else:
            outs[0][kept] = total
            kept += 1


def add(keep, came, bit, after=()):
    count, own, extent = keep.shape
    fb = block_of(extent, 2048 if count < 4 else 1024)
    block = pl.BlockSpec((count, own, fb), lambda i: (0, 0, i))
    parts = 2 if bit else 1
    out = pl.BlockSpec((count // parts, own, fb), lambda i: (0, 0, i))
    return call(
        functools.partial(add_kernel, bit),
        (extent // fb,),
        [block, block],
        [out] * parts,
        [jax.ShapeDtypeStruct((count // parts, own, extent), BF16)] * parts,
        [keep, came],
        cost=cost(count * own * extent, 6 * count * own * extent),
        after=after,
    )


def join_kernel(picks, *refs):
    for at, (i, j) in enumerate(picks):
        refs[-1][at] = refs[i][j]


def join(arrays, picks, after=()):
    own, extent = arrays[0].shape[1:]
    fb = block_of(extent, 1024)
    return call(
        functools.partial(join_kernel, picks),
        (extent // fb,),
        [pl.BlockSpec((array.shape[0], own, fb), lambda i: (0, 0, i)) for array in arrays],
        pl.BlockSpec((len(picks), own, fb), lambda i: (0, 0, i)),
        jax.ShapeDtypeStruct((len(picks), own, extent), BF16),
        arrays,
        cost=cost(0, 4 * len(picks) * own * extent),
        after=after,
    )


def every(*arrays):
    return [(i, j) for i, array in enumerate(arrays) for j in range(array.shape[0])]


def stack_kernel(count, *refs):
    for out in refs[count:]:
        for at in range(out.shape[0]):
            out[at] = refs[at][...]


def stack(arrays, own, counts, after=(), limit=32):
    extent = arrays[0].shape[1]
    fb = block_of(extent, 2048)
    return call(
        functools.partial(stack_kernel, len(arrays)),
        (extent // fb,),
        [pl.BlockSpec((own, fb), lambda i: (0, i))] * len(arrays),
        [pl.BlockSpec((count, own, fb), lambda i: (0, 0, i)) for count in counts],
        [jax.ShapeDtypeStruct((count, own, extent), BF16) for count in counts],
        arrays,
        cost=cost(0, 4 * len(arrays) * own * extent),
        after=after,
        limit=limit,
    )


def weight_kernel(links, picks, held, inverse_ref, d_out_ref, *refs):
    out_ref, done_ref = refs[-2:]
    mine, other = refs[:held], refs[held : 2 * held]
    count, own, tile = d_out_ref.shape
    hidden = [None] * count
    for j in range(count // 2):
        for pair, position in ((mine, 2 * j), (other, other_core(j, links))):
            gate, up = (pair[i][at].astype(F32) for i, at in picks[j])
            hidden[position] = (gate * jax.nn.sigmoid(gate) * up).astype(BF16)
    out_ref[...] = inverse_ref[0:1, 0:1] * lax.dot_general(
        jnp.concatenate(hidden, axis=0),
        d_out_ref[...].reshape(count * own, tile),
        (((0,), (0,)), ((), ())),
        preferred_element_type=F32,
    )
    done_ref[...] = jnp.zeros_like(done_ref)


def normed_kernel(links, picks, held, first, last, inverse_ref, w_gate_ref, w_up_ref, *refs):
    total = refs[-1]
    outs = refs[2 * held + (2 if first else 3) : -1]
    mine, other = refs[:held], refs[held : 2 * held]
    mine_grad, other_grad = refs[2 * held : 2 * held + 2]
    before = None if first else refs[2 * held + 2]
    count, own = 2 * mine_grad.shape[0], mine_grad.shape[1]
    step = pl.program_id(0)

    d_gates, d_ups = [None] * count, [None] * count
    for j in range(count // 2):
        for pair, grad, position in (
            (mine, mine_grad, 2 * j),
            (other, other_grad, other_core(j, links)),
        ):
            gate, up = (pair[i][at].astype(F32) for i, at in picks[j])
            sig = jax.nn.sigmoid(gate)
            through = grad[j].astype(F32) * inverse_ref[0:1, 0:1] * sig
            d_gates[position] = (through * up * (1.0 + gate * (1.0 - sig))).astype(BF16)
            d_ups[position] = (through * gate).astype(BF16)
    contracted = (((1,), (1,)), ((), ()))
    result = lax.dot_general(
        jnp.concatenate(d_gates, axis=0), w_gate_ref[...], contracted, preferred_element_type=F32
    ) + lax.dot_general(
        jnp.concatenate(d_ups, axis=0), w_up_ref[...], contracted, preferred_element_type=F32
    )

    @pl.when(step == 0)
    def _():
        total[...] = result if first else before[...] + result

    @pl.when(step > 0)
    def _():
        total[...] += result

    @pl.when(step == pl.num_programs(0) - 1)
    def _():
        if not last:
            outs[0][...] = total[...]
        else:
            for q, out in enumerate(outs):
                out[...] = total[q * own : (q + 1) * own, :].astype(BF16)


def product_kernel(mid_ref, gain_ref, back_ref, sums_ref):
    k, own, tile = back_ref.shape
    products = squares = jnp.zeros((own, 1), F32)
    for s in range(k):
        part = slice(s * tile, (s + 1) * tile)
        middle = mid_ref[:, part].astype(F32)
        products = products + jnp.sum(
            back_ref[s].astype(F32) * gain_ref[:, part] * middle, axis=1, keepdims=True
        )
        squares = squares + jnp.sum(middle * middle, axis=1, keepdims=True)
    sums_ref[...] = place([products, squares], own)


def result_kernel(
    width, block_ref, mid_ref, norm_ref, weight_ref, gain_ref, inverse_ref, token_ref, back_ref, *refs
):
    sums_refs, out_ref = refs[:-1], refs[-1]
    k, own, tile = back_ref.shape
    sums = functools.reduce(lambda a, b: a + b, [ref[...] for ref in sums_refs])
    root = lax.rsqrt(column(sums, 1) / width + epsilon)
    product = column(sums, 0) * root / width
    inverse = inverse_ref[0:1, 0:1]
    token = place([column(token_ref, 0), column(token_ref, 1) * inverse, column(token_ref, 2) * inverse], own)
    for s in range(k):
        part = slice(s * tile, (s + 1) * tile)
        own_d_out = gradient_rows(
            block_ref[:, part].astype(F32), token, norm_ref[:, part] * weight_ref[:, part]
        )
        scaled = back_ref[s].astype(F32) * gain_ref[:, part]
        normalized = mid_ref[:, part].astype(F32) * root
        out_ref[:, part] = (own_d_out.astype(F32) + root * (scaled - normalized * product)).astype(BF16)


def local(
    block_out,
    stream_mid,
    gate_pre,
    up_pre,
    final_gain,
    mlp_gain,
    value_weight,
    returns,
    response_mask,
    w_gate,
    w_up,
    w_down,
):
    rows, cols = lax.axis_size("row"), lax.axis_size("col")
    k = rows // cols
    own, block = block_out.shape
    width = block * cols
    tile = width // rows
    units = gate_pre.shape[1]
    ordered.clear()
    where = jnp.stack([lax.axis_index("row"), lax.axis_index("col")]).astype(jnp.int32)
    smem = pl.BlockSpec(memory_space=pltpu.SMEM)
    final_gain, mlp_gain, value_weight = final_gain[None, :], mlp_gain[None, :], value_weight[None, :]

    link_bits = bits_of(rows)[1:]
    links = len(link_bits)

    def across(values, bit):
        return lax.ppermute(values, "row", [(r, r ^ bit) for r in range(rows)])

    def linked(values, i):
        pairs = [(r, r ^ link_bits[links - 1 - i if r % 2 else i]) for r in range(rows)]
        return lax.ppermute(values, "row", pairs)

    def along(values, bit):
        return lax.ppermute(values, "col", [(c, c ^ bit) for c in range(cols)])

    def exchanged(tiles):
        came = {0: tiles[0]}
        for q in range(1, rows):
            pairs = [(r, r ^ (reverse_links(q, links) if r % 2 else q)) for r in range(rows)]
            came[reverse_links(q, links) if q % 2 else q] = lax.ppermute(tiles[q], "row", pairs)
        return [came[q] for q in range(rows)]

    packed = call(
        pack_kernel,
        (1,),
        [whole((own, block)), whole((1, block)), whole((1, block))],
        whole((own + 16, block)),
        jax.ShapeDtypeStruct((own + 16, block), BF16),
        [block_out, final_gain, value_weight],
        cost=cost(block, own * block * 4),
        limit=60,
    )
    pieces = [packed] + [along(packed, d) for d in range(1, cols)]

    paired = call(
        pair_kernel,
        (1,),
        [whole((own, units)), whole((own, units)), whole((1, own))],
        whole((2, own, units + LANES)),
        jax.ShapeDtypeStruct((2, own, units + LANES), BF16),
        [gate_pre, up_pre, response_mask[None, :]],
        cost=cost(0, own * units * 8),
    )
    hop_a = linked(paired, 0)
    hop_b = linked(paired, 1)

    *tiles, token = call(
        functools.partial(out_kernel, own * rows, k, links),
        (1,),
        [smem, whole((1, own)), whole((1, own))]
        + [whole((own + 16, block))] * cols,
        [whole((own, tile))] * rows + [whole((own, LANES))],
        [jax.ShapeDtypeStruct((own, tile), BF16)] * rows + [jax.ShapeDtypeStruct((own, LANES), F32)],
        [where, returns[None, :], response_mask[None, :], *pieces],
        scratch=[pltpu.VMEM((rows, own, tile), BF16)],
        cost=cost(own * width * 10, own * width * 4),
    )
    (d_out,) = stack(exchanged(tiles), own, [rows], after=[hop_a, hop_b])

    paired, hop_a, hop_b, d_out = lax.optimization_barrier((paired, hop_a, hop_b, d_out))
    held = [paired, hop_a, hop_b, linked(hop_a, 1)]
    picks = [((i, 0), (i, 1)) for i in range(4)]
    for i in range(2, links):
        picks = picks + [tuple((at + len(held), j) for at, j in pair) for pair in picks]
        held = held + [linked(values, i) for values in held]
    others = [across(values, 1) for values in held[:3]]

    lines = units // (2 * LANES)
    sizes = [lines * 3 // 7]
    sizes = [size * 2 * LANES for size in sizes + [lines - sum(sizes)]]
    chunks = [(sum(sizes[:i]), size) for i, size in enumerate(sizes)]
    count = rows // 2

    def reduced(number):
        start, extent = chunks[number]
        fb = block_of(math.gcd(start, extent), 1024)
        keep, send = call(
            functools.partial(partial_kernel, links),
            (extent // fb,),
            [
                whole((rows, own, tile)),
                pl.BlockSpec((fb, tile), lambda i, f=start // fb: (f + i, 0)),
            ],
            [pl.BlockSpec((count, own, fb), lambda i: (0, 0, i))] * 2,
            [jax.ShapeDtypeStruct((count, own, extent), BF16)] * 2,
            [d_out, w_down],
            limit=44,
            cost=cost(2 * rows * own * tile * extent, 2 * extent * tile + 2 * rows * own * extent),
            after=waits.get((number, 0), ()),
        )
        received = across(send, 1)
        yield
        for i in range(links):
            keep, send = add(keep, received, 1, waits.get((number, 1 + i), ()))
            received = linked(send, i)
            yield
        (keep,) = add(keep, received, 0, waits.get((number, links + 1), ()))
        for i in range(links):
            came = linked(keep, i)
            yield
            keep = join([keep, came], every(keep, came), waits.get((number, links + 2 + i), ()))
        grads[number] = (keep, across(keep, 1))
        yield

    def normed(number, total):
        start, extent = chunks[number]
        first, last = number == 0, number == len(chunks) - 1
        fb = block_of(math.gcd(start, extent), 1024)
        weights = pl.BlockSpec((tile, fb), lambda i, f=start // fb: (0, f + i))
        ins = (
            [whole((8, LANES)), weights, weights]
            + [
                pl.BlockSpec((values.shape[0], own, fb), lambda i, f=start // fb: (0, 0, f + i))
                for values in held + others
            ]
            + [pl.BlockSpec((count, own, fb), lambda i: (0, 0, i))] * 2
        )
        args = [inverse, w_gate, w_up, *held, *others, *grads[number]]
        if not first:
            ins.append(whole((rows * own, tile)))
            args.append(total)
        shape, kind, parts = ((own, tile), BF16, rows) if last else ((rows * own, tile), F32, 1)
        result = call(
            functools.partial(normed_kernel, links, picks, len(held), first, last),
            (extent // fb,),
            ins,
            [whole(shape)] * parts,
            [jax.ShapeDtypeStruct(shape, kind)] * parts,
            args,
            scratch=[pltpu.VMEM((rows * own, tile), F32)],
            limit=36,
            cost=cost(
                4 * rows * own * tile * extent,
                4 * extent * tile + 6 * rows * own * extent,
                rows * own * extent,
            ),
        )
        return result if last else result[0]

    waits = {
        (1, 0): others[:3],
        (0, links): held[3:4],
    }
    grads, total = {}, None
    chains = [reduced(number) for number in range(len(chunks))]
    for step in range(2 * links + 1):
        for chain in chains:
            next(chain)
        if step == 0:
            late, _ = lax.optimization_barrier((held[3:], ordered[0]))
            others = others + [across(values, 1) for values in late]
            waits[0, links + 1] = others[3:4]
        if step == links + 1:
            inverse = call(
                inverse_kernel,
                (1,),
                [pl.BlockSpec((2, own, LANES), lambda i: (0, 0, units // LANES))] * (2 * len(held)),
                whole((8, LANES)),
                jax.ShapeDtypeStruct((8, LANES), F32),
                [*held, *others],
                cost=cost(0, rows * own * LANES * 4),
            )
    next(chains[0])
    total = normed(0, total)
    for chain in chains[1:]:
        next(chain)
    for number in range(1, len(chunks)):
        total = normed(number, total)

    keep, send = call(
        functools.partial(arrange_kernel, k, links),
        (1,),
        [smem] + [whole((own, tile))] * rows,
        [whole((count, own, tile))] * 2,
        [jax.ShapeDtypeStruct((count, own, tile), BF16)] * 2,
        [where, *exchanged(total)],
        scratch=[pltpu.VMEM((rows, own, tile), BF16)],
        cost=cost(0, rows * own * tile * 4),
    )
    half = units // 2
    fb = block_of(half, 1024)
    blocks = half // fb
    d_w_down = None
    col_bits = bits_of(cols)
    for at, bit in enumerate(col_bits):
        received = along(send, bit)
        if at < 2:
            ins = [whole((8, LANES)), whole((rows, own, tile))] + [
                pl.BlockSpec((values.shape[0], own, fb), lambda i, at=at: (0, 0, at * blocks + i))
                for values in held + others
            ]
            args = [inverse, d_out, *held, *others]
            aliases = {}
            if at:
                ins.append(pl.BlockSpec(memory_space=pl.ANY))
                args.append(d_w_down)
                aliases = {len(args) - 1: 0}
            d_w_down, _ = call(
                functools.partial(weight_kernel, links, picks, len(held)),
                (blocks,),
                ins,
                [pl.BlockSpec((fb, tile), lambda i, at=at: (at * blocks + i, 0)), whole((8, LANES))],
                [jax.ShapeDtypeStruct((units, tile), F32), jax.ShapeDtypeStruct((8, LANES), F32)],
                args,
                cost=cost(
                    2 * rows * own * tile * half,
                    4 * half * tile + 4 * rows * own * half,
                    rows * own * half,
                ),
                aliases=aliases,
                limit=36,
            )
        if bit == col_bits[-1]:
            (total,) = add(keep, received, 0)
        else:
            keep, send = add(keep, received, k)

    row_spec, gain_spec = whole((own, block)), whole((1, block))
    sums_spec, back_spec = whole((own, LANES)), whole((k, own, tile))
    sums = call(
        product_kernel,
        (1,),
        [row_spec, gain_spec, back_spec],
        sums_spec,
        jax.ShapeDtypeStruct((own, LANES), F32),
        [stream_mid, mlp_gain, total],
        cost=cost(own * block * 5, own * block * 4),
    )
    gradient = call(
        functools.partial(result_kernel, width),
        (1,),
        [row_spec, row_spec] + [gain_spec] * 3 + [whole((8, LANES)), sums_spec, back_spec] + [sums_spec] * cols,
        row_spec,
        jax.ShapeDtypeStruct((own, block), BF16),
        [block_out, stream_mid, final_gain, value_weight, mlp_gain, inverse, token, total, sums]
        + [along(sums, d) for d in range(1, cols)],
        cost=cost(own * block * 14, own * block * 8),
    )
    return (gradient, d_w_down)


def solution(mesh):
    placed = (
        P("row", "col"),
        P("row", "col"),
        P("row", "col"),
        P("row", "col"),
        P("col"),
        P("col"),
        P("col"),
        P("row"),
        P("row"),
        P("row", "col"),
        P("row", "col"),
        P("col", "row"),
    )
    return jax.shard_map(
        local,
        mesh=mesh,
        in_specs=placed,
        out_specs=(P("row", "col"), P("col", "row")),
        check_vma=False,
    )
```
